32 devices in a mesh: row: 8 (over z, core), col: 4 (over y, x).
Axes of the slice: x: 2, y: 2, z: 4, core: 2. Of those that a mesh axis runs over, the one named last changes fastest.
Arguments:
- work: float32 [4096, 2048], P('row', 'col'), may hold values from -6 to 6
- a_tiles: bfloat16 [8, 8, 512, 512], P('row', None, 'col'), may hold values from -0.078125 to 0.078125
- b_tiles: bfloat16 [4, 4, 512, 512], P(None, 'col', 'row'), may hold values from -0.078125 to 0.078125
- u_powers: float32 [8, 3, 512, 512], P('row', None, 'col'), may hold values from -1 to 1, as said below
- v_powers: float32 [4, 3, 512, 512], P('col', None, 'row'), may hold values from -1 to 1, as said below
- shift: float32 [1], replicated, may hold values from 0.5 to 2
Outputs:
- progress: float32 [4096, 2048], P('row', 'col')
The draws below stay inside these ranges and needn't reach their ends.
Inputs may be any that keep to these rules, and one draw needn't show every extreme that they name: u_powers[i] holds U, U^2 and U^4 for a lower triangular U whose diagonal entries have magnitudes 0.3 to 0.9. v_powers[j] holds V, V^2 and V^4 for an upper triangular V whose diagonal entries have magnitudes 0.3 to 0.9.
All inputs are finite; a program needn't handle non-finite values.
Results may differ from the reference program's by a relative error of at most 0.0023.
Values may be sent and summed in bfloat16 or wider, within the bound.
A program may use at most 128 MiB of HBM per device.

```python
import math
import jax
import jax.numpy as jnp
import numpy as np
from jax import lax

T_SIZE = 512
FRONTS = 3
TROWS = 8
TCOLS = 4
FIRST = 3


def triangle_stack(key, count, lower):
    first_key, second_key, third_key = jax.random.split(key, 3)
    magnitude = jax.random.uniform(first_key, (count, T_SIZE), jnp.float32, 0.3, 0.85)
    signs = jnp.where(jax.random.bernoulli(second_key, 0.5, (count, T_SIZE)), 1.0, -1.0)
    spread = jax.random.normal(third_key, (count, T_SIZE, T_SIZE), jnp.float32) * (0.3 / jnp.sqrt(1.0 * T_SIZE))
    spread = jnp.clip(spread, -6.0 * 0.3 / jnp.sqrt(1.0 * T_SIZE), 6.0 * 0.3 / jnp.sqrt(1.0 * T_SIZE))
    identity = jnp.eye(T_SIZE, dtype=jnp.float32)
    if lower:
        strict = jnp.tril(spread, -1)
    else:
        strict = jnp.triu(spread, 1)
    base = strict + (magnitude * signs)[:, :, None] * identity[None]
    square = jnp.einsum('nab,nbc->nac', base, base, precision=lax.Precision.HIGHEST)
    fourth = jnp.einsum('nab,nbc->nac', square, square, precision=lax.Precision.HIGHEST)
    return jnp.stack([base, square, fourth], axis=1)


def draw_u_powers(key, part):
    return triangle_stack(jax.random.fold_in(key, 11), TROWS, True)


def draw_v_powers(key, part):
    return triangle_stack(jax.random.fold_in(key, 23), TCOLS, False)


def block_scale(own_key, extent, cuts, low, largest):
    def one(axis_at, parts):
        heights = jax.random.uniform(jax.random.fold_in(jax.random.fold_in(own_key, 6), axis_at), (parts,), jnp.float32, low / len(cuts), largest / len(cuts))
        return jnp.repeat(jnp.exp(heights), extent[axis_at] // parts).reshape((-1,) + (1,) * (len(extent) - axis_at - 1))

    gain = one(*cuts[0])
    for cut in cuts[1:]:
        gain = gain * one(*cut)
    return gain


def scatter_about(rng, shape, scale, most, cuts=(), kind=jnp.bfloat16):
    loudness = block_scale(rng, shape, cuts, -0.22, 0.18) if cuts else 1.0
    values = jax.random.normal(rng, shape, jnp.float32) * scale * loudness
    return jnp.minimum(jnp.maximum(values, -most), most).astype(kind)


def setup_inputs(seed: int = 0) -> dict:
    streams_of = jax.random.split(jax.random.key(seed), 7)
    return {
        "work": scatter_about(streams_of[0], (TROWS * T_SIZE, TCOLS * T_SIZE), 1.0, 6.0, ((0, 8), (1, 4)), jnp.float32),
        "a_tiles": scatter_about(streams_of[1], (TROWS, TROWS, T_SIZE, T_SIZE), (4 * T_SIZE * FRONTS) ** -0.5, 0.078125, ((0, 8), (2, 4))),
        "b_tiles": scatter_about(streams_of[2], (TCOLS, TCOLS, T_SIZE, T_SIZE), (4 * T_SIZE * FRONTS) ** -0.5, 0.078125, ((1, 4), (2, 8))),
        "u_powers": draw_u_powers(jax.random.fold_in(streams_of[6], 71), 0),
        "v_powers": draw_v_powers(jax.random.fold_in(streams_of[6], 71), 0),
        "shift": jnp.clip(jnp.exp(jax.random.uniform(streams_of[5], (1,), jnp.float32, math.log(0.5), math.log(2.0))), 0.5, 2.0),
    }


finest = lax.Precision.HIGHEST


def solve_tiles(source, u_stack, v_stack, shift_value):
    identity = jnp.eye(T_SIZE, dtype=jnp.float32)
    left_factor = identity - u_stack[:, 0]
    right_factor = identity - v_stack[:, 0]
    current = jnp.einsum("nab,nbc->nac", left_factor, source, precision=finest)
    current = jnp.einsum("nab,nbc->nac", current, right_factor, precision=finest) / (2.0 * shift_value)
    for power in range(3):
        moved = jnp.einsum("nab,nbc->nac", u_stack[:, power], current, precision=finest)
        current = current + jnp.einsum("nab,nbc->nac", moved, v_stack[:, power], precision=finest)
    return current


def rounded(values):
    narrow = lax.optimization_barrier(values.astype(jnp.bfloat16))
    return narrow.astype(jnp.float32)


def reference(work, a_tiles, b_tiles, u_powers, v_powers, shift):
    state = work.reshape(TROWS, T_SIZE, TCOLS, T_SIZE).transpose(0, 2, 1, 3)
    a_full = a_tiles.astype(jnp.float32)
    b_full = b_tiles.astype(jnp.float32)
    front_map = np.arange(TROWS)[:, None] + np.arange(TCOLS)[None, :]
    for number in range(FRONTS):
        front = FIRST + number
        row_list = [place for place in range(TROWS) if 0 <= front - place < TCOLS]
        row_index = np.array(row_list, dtype=np.int32)
        col_index = (front - row_index).astype(np.int32)
        solved = solve_tiles(state[row_index, col_index], u_powers[row_index], v_powers[col_index], shift[0])
        state = state.at[row_index, col_index].set(solved)
        down_rows = front - np.arange(TCOLS)
        valid_down = (down_rows >= 0) & (down_rows < TROWS)
        down_rows = np.clip(down_rows, 0, TROWS - 1).astype(np.int32)
        across_cols = front - np.arange(TROWS)
        valid_across = (across_cols >= 0) & (across_cols < TCOLS)
        across_cols = np.clip(across_cols, 0, TCOLS - 1).astype(np.int32)
        down_tiles = rounded(state[down_rows, np.arange(TCOLS)])
        across_tiles = rounded(state[np.arange(TROWS), across_cols])
        term_a = jnp.einsum("ijab,jbc->ijac", a_full[:, down_rows], down_tiles, precision=finest)
        term_b = jnp.einsum("iab,ijbc->ijac", across_tiles, b_full[across_cols], precision=finest)
        term = jnp.where(valid_down[None, :, None, None], term_a, 0.0) + jnp.where(valid_across[:, None, None, None], term_b, 0.0)
        state = jnp.where((front_map > front)[:, :, None, None], state - term, state)
    return state.transpose(0, 2, 1, 3).reshape(TROWS * T_SIZE, TCOLS * T_SIZE)
```

```python
import functools
import jax
import jax.numpy as jnp
from jax import lax
from jax.experimental import pallas as pl
from jax.experimental.pallas import tpu as pltpu
from jax.sharding import PartitionSpec as P

FRONTS = 3
CHUNKS = 4
MESH = pl.DeviceIdType.MESH
BF = jnp.bfloat16
F32 = jnp.float32


def dot(left, right):
    return jnp.dot(left, right, preferred_element_type=F32)


def split(value):
    high = value.astype(BF)
    return high, (value - high.astype(F32)).astype(BF)


def product(left, right):
    (lh, ll), (rh, rl) = left, right
    return dot(lh, rh) + (dot(lh, rl) + dot(ll, rh))


def kernel(rows, cols, first, work, a, b, u, v, shift, out,
           s, ubuf, vbuf, uh, ul, vh, vl, yh, yl, xs, abuf, bbuf, xd, xa,
           loc, usend, urecv, vsend, vrecv, asend, arecv, aloc, bsend, brecv, bloc,
           dsend, xsend, fsend, xdrecv, xarecv):
    r = lax.axis_index("row")
    c = lax.axis_index("col")
    width = s.shape[0]
    half = width // 2
    hr = u.shape[2]
    hv = v.shape[2]
    ch = width // CHUNKS
    mine = r + c - first
    solver = (mine >= 0) & (mine < FRONTS)
    even = lax.rem(r, 2) == 0

    def remote(src, dst, ssem, rsem, to_row, to_col):
        return pltpu.make_async_remote_copy(
            src_ref=src, dst_ref=dst, send_sem=ssem, recv_sem=rsem,
            device_id=(to_row, to_col), device_id_type=MESH)

    def arrived(ref, sem):
        pltpu.make_async_copy(ref, ref, sem).wait()

    def span(count, body):
        def step(at, carry):
            body(at)
            return carry
        lax.fori_loop(0, count, step, 0)

    own_u = pl.ds(pl.multiple_of(c * hr, hr), hr)
    own_v = pl.ds(pl.multiple_of(r * hv, hv), hv)
    lo_half, hi_half = pl.ds(0, half), pl.ds(half, half)

    load_s = pltpu.make_async_copy(work, s, loc.at[0])
    load_u = pltpu.make_async_copy(u.at[0, 0], ubuf.at[own_u], loc.at[1])
    load_v = pltpu.make_async_copy(v.at[0, 0], vbuf.at[own_v], loc.at[2])
    load_s.start()

    @pl.when(solver)
    def _():
        load_u.start()
        load_v.start()

    barrier = pltpu.get_barrier_semaphore()

    def greet_row(at):
        @pl.when(at != r)
        def _():
            pl.semaphore_signal(barrier, inc=1, device_id=(at, c), device_id_type=MESH)

    def greet_col(at):
        @pl.when(at != c)
        def _():
            pl.semaphore_signal(barrier, inc=1, device_id=(r, at), device_id_type=MESH)

    span(rows, greet_row)
    span(cols, greet_col)
    pl.semaphore_wait(barrier, rows + cols - 2)

    def factors(act):
        def step(f):
            j = first + f - r

            @pl.when((j >= 0) & (j < cols) & (j != c))
            def _():
                act(remote(u.at[0, 0, :, lo_half], ubuf.at[own_u, lo_half],
                           usend.at[f, 0], urecv.at[c, 0], r, j))

                @pl.when(c * hr + hr > half)
                def _():
                    act(remote(u.at[0, 0, :, hi_half], ubuf.at[own_u, hi_half],
                               usend.at[f, 1], urecv.at[c, 1], r, j))

            i = first + f - c

            @pl.when((i >= 0) & (i < rows) & (i != r))
            def _():
                act(remote(v.at[0, 0, :, hi_half], vbuf.at[own_v, hi_half],
                           vsend.at[f, 1], vrecv.at[r, 1], i, c))

                @pl.when(r * hv < half)
                def _():
                    act(remote(v.at[0, 0, :, lo_half], vbuf.at[own_v, lo_half],
                               vsend.at[f, 0], vrecv.at[r, 0], i, c))
        span(FRONTS, step)

    def tiles(act, act_local):
        def step(f):
            def a_step(at):
                j = lax.rem(c + 1 + at, cols)
                k = first + f - j
                need = (r + j > first + f) & (k >= 0)

                @pl.when(need & (j != c))
                def _():
                    act(remote(a.at[0, k], abuf.at[f, own_u], asend.at[f, j], arecv.at[f, c], r, j))

                @pl.when(need & (j == c))
                def _():
                    act_local(pltpu.make_async_copy(a.at[0, k], abuf.at[f, own_u], aloc.at[f]))

            def b_step(l):
                i = first + f - l
                need = (i >= 0) & (i < rows) & (c > l)

                @pl.when(need & (i != r))
                def _():
                    act(remote(b.at[l, 0], bbuf.at[f, own_v], bsend.at[f, l], brecv.at[f, r], i, c))

                @pl.when(need & (i == r))
                def _():
                    act_local(pltpu.make_async_copy(b.at[l, 0], bbuf.at[f, own_v], bloc.at[f]))

            span(cols, a_step)
            span(cols, b_step)
        span(FRONTS, step)

    factors(lambda copy: copy.start())
    tiles(lambda copy: copy.start(), lambda copy: copy.start())
    load_s.wait()

    @pl.when(solver)
    def _():
        load_u.wait()
        load_v.wait()

        def u_wait(at):
            @pl.when(at != c)
            def _():
                place = pl.ds(pl.multiple_of(at * hr, hr), hr)
                arrived(ubuf.at[place, lo_half], urecv.at[at, 0])

                @pl.when(at * hr + hr > half)
                def _():
                    arrived(ubuf.at[place, hi_half], urecv.at[at, 1])

        def v_wait(at):
            @pl.when(at != r)
            def _():
                place = pl.ds(pl.multiple_of(at * hv, hv), hv)
                arrived(vbuf.at[place, hi_half], vrecv.at[at, 1])

                @pl.when(at * hv < half)
                def _():
                    arrived(vbuf.at[place, lo_half], vrecv.at[at, 0])

        span(cols, u_wait)
        span(rows, v_wait)

        def put(high, low, power, row_part, col_part, value):
            high[power, row_part, col_part], low[power, row_part, col_part] = split(value)

        t, e = slice(0, half), slice(half, width)
        for high, low, buf, corner in ((uh, ul, ubuf, (e, t)), (vh, vl, vbuf, (t, e))):
            for part in ((t, t), (e, e), corner):
                put(high, low, 0, *part, buf[part])
            for power in range(2):
                def get(part):
                    return high[(power,) + part], low[(power,) + part]
                for part in ((t, t), (e, e)):
                    put(high, low, power + 1, *part, product(get(part), get(part)))
                x, y = corner
                put(high, low, power + 1, x, y,
                    product(get((x, x)), get((x, y))) + product(get((x, y)), get((y, y))))

    def chunk(k):
        return pl.ds(pl.multiple_of(k * ch, ch), ch)

    def forwards(f, k, act):
        part = xd.at[f, chunk(k)]

        @pl.when(even)
        def _():
            act(remote(part, part, fsend.at[f, k, 0], xdrecv.at[f, k], r + 1, c))

            @pl.when(r + 2 < rows)
            def _():
                act(remote(part, part, fsend.at[f, k, 1], xdrecv.at[f, k], r + 2, c))

    def a_needed(f):
        return (mine > f) & (first + f - c >= 0)

    def b_needed(f):
        return (mine > f) & (first + f - r >= 0)

    def update(f):
        @pl.when(a_needed(f))
        def _():
            arrived(abuf.at[f, own_u], aloc.at[f])

            def a_wait(at):
                @pl.when(at != c)
                def _():
                    arrived(abuf.at[f, pl.ds(pl.multiple_of(at * hr, hr), hr)], arecv.at[f, at])

            def x_wait(k):
                arrived(xd.at[f, chunk(k)], xdrecv.at[f, k])
                forwards(f, k, lambda copy: copy.start())

            span(cols, a_wait)
            span(CHUNKS, x_wait)
            s[...] -= dot(abuf[f], xd[f])

        @pl.when(b_needed(f))
        def _():
            arrived(bbuf.at[f, own_v], bloc.at[f])

            def b_wait(at):
                @pl.when(at != r)
                def _():
                    arrived(bbuf.at[f, pl.ds(pl.multiple_of(at * hv, hv), hv)], brecv.at[f, at])

            span(rows, b_wait)
            span(CHUNKS, lambda k: arrived(xa.at[f, chunk(k)], xarecv.at[f, k]))
            s[...] -= dot(xa[f], bbuf[f])

    span(FRONTS, update)

    def spread(k, act):
        part = xs.at[chunk(k)]
        there, beside = xd.at[mine, chunk(k)], xa.at[mine, chunk(k)]

        @pl.when(r + 1 < rows)
        def _():
            act(remote(part, there, dsend.at[k, 0], xdrecv.at[mine, k], r + 1, c))

        def across(at):
            j = c + 1 + at

            @pl.when(j < cols)
            def _():
                act(remote(part, beside, xsend.at[k, at], xarecv.at[mine, k], r, j))

        span(cols - 1, across)

        @pl.when(even & (r + 2 < rows))
        def _():
            act(remote(part, there, dsend.at[k, 1], xdrecv.at[mine, k], r + 2, c))

    @pl.when(solver)
    def _():
        inverse = 0.5 / jnp.broadcast_to(shift[0], (1, width)).astype(F32)
        for part, extent in ((slice(0, half), half), (slice(half, width), width)):
            now = s[part, :]
            yh[0, part, :], yl[0, part, :] = split(now)
            for stage in range(FRONTS + 1):
                power = max(stage - 1, 0)
                moved = product((uh[power, part, :extent], ul[power, part, :extent]),
                                (yh[stage, :extent, :], yl[stage, :extent, :]))
                if stage == 0:
                    moved = now - moved
                mh, ml = split(moved)
                left = product((mh[:, :half], ml[:, :half]),
                               (vh[power, :half, :half], vl[power, :half, :half]))
                right = product((mh, ml), (vh[power, :, half:], vl[power, :, half:]))
                turned = jnp.concatenate([left, right], axis=1)
                now = (moved - turned) * inverse if stage == 0 else now + turned
                if stage < FRONTS:
                    yh[stage + 1, part, :], yl[stage + 1, part, :] = split(now)
            s[part, :] = now
            xs[part, :] = now.astype(BF)
            for k in range(CHUNKS):
                if part.start <= k * ch < part.stop:
                    spread(k, lambda copy: copy.start())

    store = pltpu.make_async_copy(s, out, loc.at[0])
    store.start()
    factors(lambda copy: copy.wait_send())
    tiles(lambda copy: copy.wait_send(), lambda copy: None)

    def drain(f):
        @pl.when(a_needed(f))
        def _():
            span(CHUNKS, lambda k: forwards(f, k, lambda copy: copy.wait_send()))

    span(FRONTS, drain)

    @pl.when(solver)
    def _():
        span(CHUNKS, lambda k: spread(k, lambda copy: copy.wait_send()))

    store.wait()


def per_device(rows, cols, work, a, b, u, v, shift):
    first = max(0, (rows + cols) // 2 - FRONTS)
    width = work.shape[0]
    tile = (width, width)
    any_ref = pl.BlockSpec(memory_space=pl.ANY)
    dma = pltpu.SemaphoreType.DMA
    stack = [pltpu.VMEM((FRONTS,) + tile, BF)]
    return pl.pallas_call(
        functools.partial(kernel, rows, cols, first),
        out_shape=jax.ShapeDtypeStruct(work.shape, work.dtype),
        in_specs=[any_ref] * 5 + [pl.BlockSpec(memory_space=pltpu.SMEM)],
        out_specs=any_ref,
        scratch_shapes=[pltpu.VMEM(tile, F32)] * 3 + stack * 4
        + [pltpu.VMEM((FRONTS + 1,) + tile, BF)] * 2
        + [pltpu.VMEM(tile, BF)] + stack * 4
        + [dma((3,)), dma((FRONTS, 2)), dma((cols, 2)), dma((FRONTS, 2)), dma((rows, 2)),
           dma((FRONTS, cols)), dma((FRONTS, cols)), dma((FRONTS,)),
           dma((FRONTS, cols)), dma((FRONTS, rows)), dma((FRONTS,)),
           dma((CHUNKS, 2)), dma((CHUNKS, cols - 1)), dma((FRONTS, CHUNKS, 2)),
           dma((FRONTS, CHUNKS)), dma((FRONTS, CHUNKS))],
        compiler_params=pltpu.CompilerParams(
            collective_id=0, has_side_effects=True, vmem_limit_bytes=48 * 1024 * 1024),
    )(work, a, b, u, v, shift)


def solution(mesh):
    placed = (
        P("row", "col"),
        P("row", None, "col", None),
        P(None, "col", "row", None),
        P("row", None, "col", None),
        P("col", None, "row", None),
        P(),
    )
    return jax.shard_map(
        functools.partial(per_device, mesh.shape["row"], mesh.shape["col"]),
        mesh=mesh, in_specs=placed, out_specs=P("row", "col"), check_vma=False
    )
```

```python
import functools
import jax
import jax.numpy as jnp
from jax import lax
from jax.experimental import pallas as pl
from jax.experimental.pallas import tpu as pltpu
from jax.sharding import PartitionSpec as P

FRONTS = 3
CHUNKS = 8
LANES = 128
MESH = pl.DeviceIdType.MESH
BF = jnp.bfloat16
F32 = jnp.float32


def dot(left, right):
    return jnp.dot(left, right, preferred_element_type=F32)


def split(value):
    high = value.astype(BF)
    return high, (value - high.astype(F32)).astype(BF)


def product(left, right):
    (lh, ll), (rh, rl) = left, right
    return dot(lh, rh) + (dot(lh, rl) + dot(ll, rh))


def kernel(rows, cols, first, work, a, b, u, v, shift, out,
           s, ubuf, vbuf, uh, ul, vh, vl, yh, yl, xs, abuf, bbuf, xd, xa,
           loc, usend, urecv, vsend, vrecv, asend, arecv, aloc, bsend, brecv, bloc,
           dsend, xsend, fsend, xdrecv, xarecv):
    r = lax.axis_index("row")
    c = lax.axis_index("col")
    width = s.shape[0]
    half = width // 2
    hr = u.shape[2]
    hv = v.shape[2]
    ch = width // CHUNKS
    mine = r + c - first
    solver = (mine >= 0) & (mine < FRONTS)
    even = lax.rem(r, 2) == 0
    last = mine == FRONTS - 1
    blocks = width // LANES

    def remote(src, dst, ssem, rsem, to_row, to_col):
        return pltpu.make_async_remote_copy(
            src_ref=src, dst_ref=dst, send_sem=ssem, recv_sem=rsem,
            device_id=(to_row, to_col), device_id_type=MESH)

    def arrived(ref, sem):
        pltpu.make_async_copy(ref, ref, sem).wait()

    def span(count, body):
        def step(at, carry):
            body(at)
            return carry
        lax.fori_loop(0, count, step, 0)

    own_u = pl.ds(pl.multiple_of(c * hr, hr), hr)
    own_v = pl.ds(pl.multiple_of(r * hv, hv), hv)

    load_s = pltpu.make_async_copy(work, s, loc.at[0])
    load_u = pltpu.make_async_copy(u.at[0, 0], ubuf.at[own_u], loc.at[1])
    load_v = pltpu.make_async_copy(v.at[0, 0], vbuf.at[own_v], loc.at[2])
    load_s.start()

    @pl.when(solver)
    def _():
        for low in range(blocks):
            for high in range(low + 1, blocks):
                if low * LANES // half == high * LANES // half:
                    x, y = pl.ds(low * LANES, LANES), pl.ds(high * LANES, LANES)
                    ubuf[x, y] = jnp.zeros((LANES, LANES), F32)
                    vbuf[y, x] = jnp.zeros((LANES, LANES), F32)
        load_u.start()
        load_v.start()

    barrier = pltpu.get_barrier_semaphore()

    def greet_row(at):
        @pl.when(at != r)
        def _():
            pl.semaphore_signal(barrier, inc=1, device_id=(at, c), device_id_type=MESH)

    def greet_col(at):
        @pl.when(at != c)
        def _():
            pl.semaphore_signal(barrier, inc=1, device_id=(r, at), device_id_type=MESH)

    span(rows, greet_row)
    span(cols, greet_col)
    pl.semaphore_wait(barrier, rows + cols - 2)

    def u_filled(at, body):
        reach = (at * hr + hr - 1) // LANES
        for block in range(blocks):
            @pl.when(reach == block)
            def _():
                body(pl.ds(0, (block + 1) * LANES))

    def v_filled(at, body):
        reach = at * hv // LANES
        for block in range(blocks):
            @pl.when(reach == block)
            def _():
                body(pl.ds(block * LANES, width - block * LANES))

    def factors(f, act):
        j = first + f - r

        @pl.when((j >= 0) & (j < cols) & (j != c))
        def _():
            u_filled(c, lambda part: act(remote(
                u.at[0, 0, :, part], ubuf.at[own_u, part], usend.at[f], urecv.at[c], r, j)))

        i = first + f - c

        @pl.when((i >= 0) & (i < rows) & (i != r))
        def _():
            v_filled(r, lambda part: act(remote(
                v.at[0, 0, :, part], vbuf.at[own_v, part], vsend.at[f], vrecv.at[r], i, c)))

    def tiles(act, act_local):
        def step(f):
            def a_step(at):
                j = lax.rem(c + 1 + at, cols)
                k = first + f - j
                need = (r + j > first + f) & (k >= 0)

                @pl.when(need & (j != c))
                def _():
                    act(remote(a.at[0, k], abuf.at[f, own_u], asend.at[f, j], arecv.at[f, c], r, j))

                @pl.when(need & (j == c))
                def _():
                    act_local(pltpu.make_async_copy(a.at[0, k], abuf.at[f, own_u], aloc.at[f]))

            def b_step(l):
                i = first + f - l
                need = (i >= 0) & (i < rows) & (c > l)

                @pl.when(need & (i != r))
                def _():
                    act(remote(b.at[l, 0], bbuf.at[f, own_v], bsend.at[f, l], brecv.at[f, r], i, c))

                @pl.when(need & (i == r))
                def _():
                    act_local(pltpu.make_async_copy(b.at[l, 0], bbuf.at[f, own_v], bloc.at[f]))

            span(cols, a_step)
            span(cols, b_step)
        span(FRONTS, step)

    factors(0, lambda copy: copy.start())
    load_s.wait()
    factors(0, lambda copy: copy.wait_send())
    for f in range(1, FRONTS):
        factors(f, lambda copy: copy.start())

    t, e = slice(0, half), slice(half, width)

    def prepare(high, low, buf, corner, scale):
        x, y = corner

        def put(slot, part, value):
            high[(slot,) + part], low[(slot,) + part] = split(value)

        def get(slot, part):
            return high[(slot,) + part], low[(slot,) + part]

        def square(slot, part):
            if part != corner:
                return product(get(slot, part), get(slot, part))
            return (product(get(slot, (x, x)), get(slot, corner))
                    + product(get(slot, corner), get(slot, (y, y))))

        parts = ((t, t), (e, e), corner)
        eye = (lax.broadcasted_iota(jnp.int32, (half, half), 0)
               == lax.broadcasted_iota(jnp.int32, (half, half), 1)).astype(F32)
        for part in parts:
            put(4, part, buf[part])
        for part in parts:
            base = buf[part]
            put(0, part, ((eye - base) if part != corner else -base) * scale)
        for part in parts:
            value = square(4, part)
            put(2, part, value)
            put(1, part, (buf[part] - value) * scale)
        for part in parts:
            put(3, part, square(2, part))

    @pl.when(solver)
    def _():
        load_u.wait()

        def u_wait(at):
            @pl.when(at != c)
            def _():
                place = pl.ds(pl.multiple_of(at * hr, hr), hr)
                u_filled(at, lambda part: arrived(ubuf.at[place, part], urecv.at[at]))

        span(cols, u_wait)
        prepare(uh, ul, ubuf, (e, t), 1.0)

    for f in range(1, FRONTS):
        factors(f, lambda copy: copy.wait_send())
    tiles(lambda copy: copy.start(), lambda copy: copy.start())

    @pl.when(solver)
    def _():
        load_v.wait()

        def v_wait(at):
            @pl.when(at != r)
            def _():
                place = pl.ds(pl.multiple_of(at * hv, hv), hv)
                v_filled(at, lambda part: arrived(vbuf.at[place, part], vrecv.at[at]))

        span(rows, v_wait)
        prepare(vh, vl, vbuf, (t, e), 0.5 / jnp.broadcast_to(shift[0], (1, half)).astype(F32))

    def chunk(k):
        return pl.ds(pl.multiple_of(k * ch, ch), ch)

    def forwards(f, k, act):
        part = xd.at[f, chunk(k)]

        @pl.when(even)
        def _():
            act(remote(part, part, fsend.at[f, k, 0], xdrecv.at[f, k], r + 1, c))

            @pl.when(r + 2 < rows)
            def _():
                act(remote(part, part, fsend.at[f, k, 1], xdrecv.at[f, k], r + 2, c))

    def a_needed(f):
        return (mine > f) & (first + f - c >= 0)

    def b_needed(f):
        return (mine > f) & (first + f - r >= 0)

    def update(f):
        @pl.when(a_needed(f))
        def _():
            arrived(abuf.at[f, own_u], aloc.at[f])

            def a_wait(at):
                @pl.when(at != c)
                def _():
                    arrived(abuf.at[f, pl.ds(pl.multiple_of(at * hr, hr), hr)], arecv.at[f, at])

            def x_wait(k):
                arrived(xd.at[f, chunk(k)], xdrecv.at[f, k])
                forwards(f, k, lambda copy: copy.start())

            span(cols, a_wait)
            span(CHUNKS, x_wait)
            s[...] -= dot(abuf[f], xd[f])

        @pl.when(b_needed(f))
        def _():
            arrived(bbuf.at[f, own_v], bloc.at[f])

            def b_wait(at):
                @pl.when(at != r)
                def _():
                    arrived(bbuf.at[f, pl.ds(pl.multiple_of(at * hv, hv), hv)], brecv.at[f, at])

            span(rows, b_wait)
            span(CHUNKS, lambda k: arrived(xa.at[f, chunk(k)], xarecv.at[f, k]))
            s[...] -= dot(xa[f], bbuf[f])

    span(FRONTS, update)

    def urgent(k, act):
        part = xs.at[chunk(k)]

        @pl.when(r + 1 < rows)
        def _():
            act(remote(part, xd.at[mine, chunk(k)], dsend.at[k, 0], xdrecv.at[mine, k], r + 1, c))

        @pl.when(c + 1 < cols)
        def _():
            act(remote(part, xa.at[mine, chunk(k)], xsend.at[k, 0], xarecv.at[mine, k], r, c + 1))

    def others(k, act):
        part = xs.at[chunk(k)]

        @pl.when(even & (r + 2 < rows))
        def _():
            act(remote(part, xd.at[mine, chunk(k)], dsend.at[k, 1], xdrecv.at[mine, k], r + 2, c))

        def across(at):
            @pl.when(c + at < cols)
            def _():
                act(remote(part, xa.at[mine, chunk(k)], xsend.at[k, at - 1],
                           xarecv.at[mine, k], r, c + at))

        span(cols - 2, lambda at: across(at + 2))

    def start(copy):
        copy.start()

    def sent(copy):
        copy.wait_send()

    @pl.when(solver)
    def _():
        for part, extent in ((t, half), (e, width)):
            now = s[part, :]
            yh[0, part, :], yl[0, part, :] = split(now)

            def left(slot, stage):
                return split(product((uh[slot, part, :extent], ul[slot, part, :extent]),
                                     (yh[stage, :extent, :], yl[stage, :extent, :])))

            def right(slot, moved):
                high, low = moved
                near = product((high[:, :half], low[:, :half]),
                               (vh[slot, :half, :half], vl[slot, :half, :half]))
                far = product((high, low), (vh[slot, :, half:], vl[slot, :, half:]))
                return jnp.concatenate([near, far], axis=1)

            zero, one = left(0, 0), left(1, 0)
            now = right(0, zero) + right(1, one)
            for stage in (1, 2):
                yh[stage, part, :], yl[stage, part, :] = split(now)
                now = now + right(stage + 1, left(stage + 1, stage))
            s[part, :] = now
            xs[part, :] = now.astype(BF)
            lowest = part.start // ch

            def send(at):
                urgent(lowest + at, start)

                @pl.when(last)
                def _():
                    others(lowest + at, start)

            span(CHUNKS // 2, send)

        @pl.when(jnp.logical_not(last))
        def _():
            span(CHUNKS, lambda k: urgent(k, sent))
            span(CHUNKS, lambda k: others(k, start))

    store = pltpu.make_async_copy(s, out, loc.at[0])
    store.start()
    tiles(lambda copy: copy.wait_send(), lambda copy: None)

    def drain(f):
        @pl.when(a_needed(f))
        def _():
            span(CHUNKS, lambda k: forwards(f, k, lambda copy: copy.wait_send()))

    span(FRONTS, drain)

    @pl.when(solver)
    def _():
        span(CHUNKS, lambda k: others(k, sent))

        @pl.when(last)
        def _():
            span(CHUNKS, lambda k: urgent(k, sent))

    store.wait()


def per_device(rows, cols, work, a, b, u, v, shift):
    first = max(0, (rows + cols) // 2 - FRONTS)
    width = work.shape[0]
    tile = (width, width)
    any_ref = pl.BlockSpec(memory_space=pl.ANY)
    dma = pltpu.SemaphoreType.DMA
    stack = [pltpu.VMEM((FRONTS,) + tile, BF)]
    return pl.pallas_call(
        functools.partial(kernel, rows, cols, first),
        out_shape=jax.ShapeDtypeStruct(work.shape, work.dtype),
        in_specs=[any_ref] * 5 + [pl.BlockSpec(memory_space=pltpu.SMEM)],
        out_specs=any_ref,
        scratch_shapes=[pltpu.VMEM(tile, F32)] * 3 + [pltpu.VMEM((5,) + tile, BF)] * 4
        + [pltpu.VMEM((3,) + tile, BF)] * 2
        + [pltpu.VMEM(tile, BF)] + stack * 4
        + [dma((3,)), dma((FRONTS,)), dma((cols,)), dma((FRONTS,)), dma((rows,)),
           dma((FRONTS, cols)), dma((FRONTS, cols)), dma((FRONTS,)),
           dma((FRONTS, cols)), dma((FRONTS, rows)), dma((FRONTS,)),
           dma((CHUNKS, 2)), dma((CHUNKS, cols - 1)), dma((FRONTS, CHUNKS, 2)),
           dma((FRONTS, CHUNKS)), dma((FRONTS, CHUNKS))],
        compiler_params=pltpu.CompilerParams(
            collective_id=0, has_side_effects=True, vmem_limit_bytes=63 * 1024 * 1024),
    )(work, a, b, u, v, shift)


def solution(mesh):
    placed = (
        P("row", "col"),
        P("row", None, "col", None),
        P(None, "col", "row", None),
        P("row", None, "col", None),
        P("col", None, "row", None),
        P(),
    )
    return jax.shard_map(
        functools.partial(per_device, mesh.shape["row"], mesh.shape["col"]),
        mesh=mesh, in_specs=placed, out_specs=P("row", "col"), check_vma=False
    )
```

```python
import functools
import jax
import jax.numpy as jnp
from jax import lax
from jax.experimental import pallas as pl
from jax.experimental.pallas import tpu as pltpu
from jax.sharding import PartitionSpec as P

FRONTS = 3
CHUNKS = 8
LANES = 128
MESH = pl.DeviceIdType.MESH
BF = jnp.bfloat16
F32 = jnp.float32


def dot(left, right):
    return jnp.dot(left, right, preferred_element_type=F32)


def split(value):
    high = value.astype(BF)
    return high, (value - high.astype(F32)).astype(BF)


def product(left, right):
    (lh, ll), (rh, rl) = left, right
    return dot(lh, rh) + (dot(lh, rl) + dot(ll, rh))


def kernel(rows, cols, first, work, a, b, u, v, shift, out,
           s, ubuf, vbuf, uh, ul, vh, vl, yh, yl, xs, abuf, bbuf, xd, xa,
           loc, usend, urecv, vsend, vrecv, asend, arecv, aloc, bsend, brecv, bloc,
           dsend, xsend, fsend, ssend, xdrecv, xarecv, vpass, vgot):
    r = lax.axis_index("row")
    c = lax.axis_index("col")
    width = s.shape[0]
    half = width // 2
    hr = u.shape[2]
    hv = v.shape[2]
    ch = width // CHUNKS
    mine = r + c - first
    solver = (mine >= 0) & (mine < FRONTS)
    even = lax.rem(r, 2) == 0
    last = mine == FRONTS - 1
    blocks = width // LANES

    def remote(src, dst, ssem, rsem, to_row, to_col):
        return pltpu.make_async_remote_copy(
            src_ref=src, dst_ref=dst, send_sem=ssem, recv_sem=rsem,
            device_id=(to_row, to_col), device_id_type=MESH)

    def arrived(ref, sem):
        pltpu.make_async_copy(ref, ref, sem).wait()

    def span(count, body):
        def step(at, carry):
            body(at)
            return carry
        lax.fori_loop(0, count, step, 0)

    own_u = pl.ds(pl.multiple_of(c * hr, hr), hr)
    own_v = pl.ds(pl.multiple_of(r * hv, hv), hv)

    load_s = pltpu.make_async_copy(work, s, loc.at[0])
    load_u = pltpu.make_async_copy(u.at[0, 0], ubuf.at[own_u], loc.at[1])
    load_v = pltpu.make_async_copy(v.at[0, 0], vbuf.at[own_v], loc.at[2])
    load_s.start()

    @pl.when(solver)
    def _():
        for low in range(blocks):
            for high in range(low + 1, blocks):
                if low * LANES // half == high * LANES // half:
                    x, y = pl.ds(low * LANES, LANES), pl.ds(high * LANES, LANES)
                    ubuf[x, y] = jnp.zeros((LANES, LANES), F32)
                    vbuf[y, x] = jnp.zeros((LANES, LANES), F32)
        load_u.start()

    @pl.when(solver & (mine != 1))
    def _():
        load_v.start()

    barrier = pltpu.get_barrier_semaphore()

    def greet_row(at):
        @pl.when(at != r)
        def _():
            pl.semaphore_signal(barrier, inc=1, device_id=(at, c), device_id_type=MESH)

    def greet_col(at):
        @pl.when(at != c)
        def _():
            pl.semaphore_signal(barrier, inc=1, device_id=(r, at), device_id_type=MESH)

    span(rows, greet_row)
    span(cols, greet_col)
    pl.semaphore_wait(barrier, rows + cols - 2)

    def u_filled(at, body):
        reach = (at * hr + hr - 1) // LANES
        for block in range(blocks):
            @pl.when(reach == block)
            def _():
                body(pl.ds(0, (block + 1) * LANES))

    def v_filled(at, body):
        reach = at * hv // LANES
        for block in range(blocks):
            @pl.when(reach == block)
            def _():
                body(pl.ds(block * LANES, width - block * LANES))

    def factors(f, act):
        j = first + f - r

        @pl.when((j >= 0) & (j < cols) & (j != c))
        def _():
            u_filled(c, lambda part: act(remote(
                u.at[0, 0, :, part], ubuf.at[own_u, part], usend.at[f], urecv.at[c], r, j)))

        i = first + f - c

        @pl.when((f != 1) & (i >= 0) & (i < rows) & (i != r))
        def _():
            v_filled(r, lambda part: act(remote(
                v.at[0, 0, :, part], vbuf.at[own_v, part], vsend.at[f], vrecv.at[r], i, c)))

    def tiles(f, near, act, act_local):
        def a_step(at):
            j = lax.rem(c + 1 + at, cols)
            k = first + f - j
            need = (r + j > first + f) & (k >= 0) & ((r + j == first + f + 1) == near)

            @pl.when(need & (j != c))
            def _():
                act(remote(a.at[0, k], abuf.at[f, own_u], asend.at[f, j], arecv.at[f, c], r, j))

            @pl.when(need & (j == c))
            def _():
                act_local(pltpu.make_async_copy(a.at[0, k], abuf.at[f, own_u], aloc.at[f]))

        def b_step(l):
            i = first + f - l
            need = (i >= 0) & (i < rows) & (c > l) & ((c == l + 1) == near)

            @pl.when(need & (i != r))
            def _():
                act(remote(b.at[l, 0], bbuf.at[f, own_v], bsend.at[f, l], brecv.at[f, r], i, c))

            @pl.when(need & (i == r))
            def _():
                act_local(pltpu.make_async_copy(b.at[l, 0], bbuf.at[f, own_v], bloc.at[f]))

        span(cols, a_step)
        span(cols, b_step)

    def start(copy):
        copy.start()

    def sent(copy):
        copy.wait_send()

    def nothing(copy):
        return None

    factors(0, start)
    load_s.wait()

    def send_ahead(paced):
        for f in range(1, FRONTS):
            if paced:
                factors(f - 1, sent)
                if f > 1:
                    tiles(f - 2, True, sent, nothing)
            factors(f, start)
            tiles(f - 1, True, start, start)
        if paced:
            factors(FRONTS - 1, sent)
            tiles(FRONTS - 2, True, sent, nothing)
        tiles(FRONTS - 1, True, start, start)
        span(FRONTS, lambda f: tiles(f, False, start, start))

    @pl.when(mine != 0)
    def _():
        send_ahead(True)

    t, e = slice(0, half), slice(half, width)

    def prepare(high, low, buf, corner, scale):
        x, y = corner

        def put(slot, part, value):
            high[(slot,) + part], low[(slot,) + part] = split(value)

        def get(slot, part):
            return high[(slot,) + part], low[(slot,) + part]

        def square(slot, part):
            if part != corner:
                return product(get(slot, part), get(slot, part))
            return (product(get(slot, (x, x)), get(slot, corner))
                    + product(get(slot, corner), get(slot, (y, y))))

        parts = ((t, t), (e, e), corner)
        eye = (lax.broadcasted_iota(jnp.int32, (half, half), 0)
               == lax.broadcasted_iota(jnp.int32, (half, half), 1)).astype(F32)
        for part in parts:
            put(4, part, buf[part])
        for part in parts:
            base = buf[part]
            put(0, part, ((eye - base) if part != corner else -base) * scale)
        for part in parts:
            value = square(4, part)
            put(2, part, value)
            put(1, part, (buf[part] - value) * scale)
        for part in parts:
            put(3, part, square(2, part))

    @pl.when(solver)
    def _():
        load_u.wait()

        def u_wait(at):
            @pl.when(at != c)
            def _():
                place = pl.ds(pl.multiple_of(at * hr, hr), hr)
                u_filled(at, lambda part: arrived(ubuf.at[place, part], urecv.at[at]))

        span(cols, u_wait)
        prepare(uh, ul, ubuf, (e, t), 1.0)

    @pl.when(mine == 0)
    def _():
        send_ahead(False)

    beside = jnp.where(even, r + 1, r - 1)
    passing = solver & (mine != 1) & ((mine == 0) == even)

    def pass_v(act):
        for at, (x, y) in enumerate(((t, t), (slice(0, width), e))):
            part = vbuf.at[pl.ds(x.start, x.stop - x.start), pl.ds(y.start, y.stop - y.start)]
            act(remote(part, part, vpass.at[at], vgot.at[at], beside, c))

    @pl.when(mine == 1)
    def _():
        pass_v(lambda copy: copy.wait_recv())

    @pl.when(solver & (mine != 1))
    def _():
        load_v.wait()

        def v_wait(at):
            @pl.when(at != r)
            def _():
                place = pl.ds(pl.multiple_of(at * hv, hv), hv)
                v_filled(at, lambda part: arrived(vbuf.at[place, part], vrecv.at[at]))

        span(rows, v_wait)

        @pl.when(passing)
        def _():
            pass_v(start)

    @pl.when(solver)
    def _():
        prepare(vh, vl, vbuf, (t, e), 0.5 / jnp.broadcast_to(shift[0], (1, half)).astype(F32))

    def chunk(k):
        return pl.ds(pl.multiple_of(k * ch, ch), ch)

    def forwards(f, k, act):
        part = xd.at[f, chunk(k)]

        @pl.when(even)
        def _():
            act(remote(part, part, fsend.at[f, k, 0], xdrecv.at[f, k], r + 1, c))

            @pl.when(r + 2 < rows)
            def _():
                act(remote(part, part, fsend.at[f, k, 1], xdrecv.at[f, k], r + 2, c))

    square = cols == 4

    def sideways(f, k, act):
        if square:
            part = xa.at[f, chunk(k)]
            source = first + f - r

            @pl.when(((source == 0) & (c == 2)) | ((source == 1) & (c == 3) & (f == FRONTS - 1)))
            def _():
                act(remote(part, part, ssend.at[f, k], xarecv.at[f, k], r, 5 - c))

    def a_needed(f):
        return (mine > f) & (first + f - c >= 0)

    def b_needed(f):
        return (mine > f) & (first + f - r >= 0)

    def update(f):
        @pl.when(a_needed(f))
        def _():
            arrived(abuf.at[f, own_u], aloc.at[f])

            def a_wait(at):
                @pl.when(at != c)
                def _():
                    arrived(abuf.at[f, pl.ds(pl.multiple_of(at * hr, hr), hr)], arecv.at[f, at])

            def x_wait(k):
                arrived(xd.at[f, chunk(k)], xdrecv.at[f, k])
                forwards(f, k, lambda copy: copy.start())

            span(cols, a_wait)
            span(CHUNKS, x_wait)
            s[...] -= dot(abuf[f], xd[f])

        @pl.when(b_needed(f))
        def _():
            arrived(bbuf.at[f, own_v], bloc.at[f])

            def b_wait(at):
                @pl.when(at != r)
                def _():
                    arrived(bbuf.at[f, pl.ds(pl.multiple_of(at * hv, hv), hv)], brecv.at[f, at])

            span(rows, b_wait)

            def x_wait(k):
                arrived(xa.at[f, chunk(k)], xarecv.at[f, k])
                sideways(f, k, start)

            span(CHUNKS, x_wait)
            s[...] -= dot(xa[f], bbuf[f])

    span(FRONTS, update)

    def spread(k, act):
        part = xs.at[chunk(k)]
        there, across = xd.at[mine, chunk(k)], xa.at[mine, chunk(k)]

        @pl.when(r + 1 < rows)
        def _():
            act(remote(part, there, dsend.at[k, 0], xdrecv.at[mine, k], r + 1, c))

        def right(at):
            relayed = (c == 0) & (at == 3) | (c == 1) & (at == 1) & last if square else at < 0

            @pl.when((c + at < cols) & jnp.logical_not(relayed))
            def _():
                act(remote(part, across, xsend.at[k, at - 1], xarecv.at[mine, k], r, c + at))

        span(cols - 1, lambda at: right(at + 1))

        @pl.when(even & (r + 2 < rows))
        def _():
            act(remote(part, there, dsend.at[k, 1], xdrecv.at[mine, k], r + 2, c))

    @pl.when(solver)
    def _():
        for part, extent in ((t, half), (e, width)):
            now = s[part, :]
            yh[0, part, :], yl[0, part, :] = split(now)

            def left(slot, stage):
                return split(product((uh[slot, part, :extent], ul[slot, part, :extent]),
                                     (yh[stage, :extent, :], yl[stage, :extent, :])))

            def right(slot, moved):
                high, low = moved
                near = product((high[:, :half], low[:, :half]),
                               (vh[slot, :half, :half], vl[slot, :half, :half]))
                far = product((high, low), (vh[slot, :, half:], vl[slot, :, half:]))
                return jnp.concatenate([near, far], axis=1)

            zero, one = left(0, 0), left(1, 0)
            now = right(0, zero) + right(1, one)
            for stage in (1, 2):
                yh[stage, part, :], yl[stage, part, :] = split(now)
                now = now + right(stage + 1, left(stage + 1, stage))
            s[part, :] = now
            xs[part, :] = now.astype(BF)
            lowest = part.start // ch

            span(CHUNKS // 2, lambda at: spread(lowest + at, start))

    store = pltpu.make_async_copy(s, out, loc.at[0])
    store.start()

    @pl.when(mine == 0)
    def _():
        for f in range(FRONTS):
            factors(f, sent)
        for f in range(FRONTS - 1):
            tiles(f, True, sent, nothing)

    tiles(FRONTS - 1, True, sent, nothing)
    span(FRONTS, lambda f: tiles(f, False, sent, nothing))

    def drain(f):
        @pl.when(a_needed(f))
        def _():
            span(CHUNKS, lambda k: forwards(f, k, sent))

        @pl.when(b_needed(f))
        def _():
            span(CHUNKS, lambda k: sideways(f, k, sent))

    span(FRONTS, drain)

    @pl.when(passing)
    def _():
        pass_v(sent)

    @pl.when(solver)
    def _():
        span(CHUNKS, lambda k: spread(k, sent))

    store.wait()


def per_device(rows, cols, work, a, b, u, v, shift):
    first = max(0, (rows + cols) // 2 - FRONTS)
    width = work.shape[0]
    tile = (width, width)
    any_ref = pl.BlockSpec(memory_space=pl.ANY)
    dma = pltpu.SemaphoreType.DMA
    stack = [pltpu.VMEM((FRONTS,) + tile, BF)]
    return pl.pallas_call(
        functools.partial(kernel, rows, cols, first),
        out_shape=jax.ShapeDtypeStruct(work.shape, work.dtype),
        in_specs=[any_ref] * 5 + [pl.BlockSpec(memory_space=pltpu.SMEM)],
        out_specs=any_ref,
        scratch_shapes=[pltpu.VMEM(tile, F32)] * 3 + [pltpu.VMEM((5,) + tile, BF)] * 4
        + [pltpu.VMEM((3,) + tile, BF)] * 2
        + [pltpu.VMEM(tile, BF)] + stack * 4
        + [dma((3,)), dma((FRONTS,)), dma((cols,)), dma((FRONTS,)), dma((rows,)),
           dma((FRONTS, cols)), dma((FRONTS, cols)), dma((FRONTS,)),
           dma((FRONTS, cols)), dma((FRONTS, rows)), dma((FRONTS,)),
           dma((CHUNKS, 2)), dma((CHUNKS, cols - 1)), dma((FRONTS, CHUNKS, 2)),
           dma((FRONTS, CHUNKS)), dma((FRONTS, CHUNKS)), dma((FRONTS, CHUNKS)), dma((2,)), dma((2,))],
        compiler_params=pltpu.CompilerParams(
            collective_id=0, has_side_effects=True, vmem_limit_bytes=63 * 1024 * 1024),
    )(work, a, b, u, v, shift)


def solution(mesh):
    placed = (
        P("row", "col"),
        P("row", None, "col", None),
        P(None, "col", "row", None),
        P("row", None, "col", None),
        P("col", None, "row", None),
        P(),
    )
    return jax.shard_map(
        functools.partial(per_device, mesh.shape["row"], mesh.shape["col"]),
        mesh=mesh, in_specs=placed, out_specs=P("row", "col"), check_vma=False
    )
```

```python
import functools
import jax
import jax.numpy as jnp
from jax import lax
from jax.experimental import pallas as pl
from jax.experimental.pallas import tpu as pltpu
from jax.sharding import PartitionSpec as P

FRONTS = 3
CHUNKS = 8
LANES = 128
MESH = pl.DeviceIdType.MESH
BF = jnp.bfloat16
F32 = jnp.float32


def dot(left, right):
    return jnp.dot(left, right, preferred_element_type=F32)


def split(value):
    high = value.astype(BF)
    return high, (value - high.astype(F32)).astype(BF)


def product(left, right):
    (lh, ll), (rh, rl) = left, right
    return dot(lh, rh) + (dot(lh, rl) + dot(ll, rh))


def kernel(rows, cols, first, work, a, b, u, v, shift, s,
           ubuf, vbuf, uh, ul, vh, vl, yh, yl, xs, abuf, bbuf, xd, xa,
           loc, usend, urecv, vsend, vrecv, asend, arecv, aloc, bsend, brecv, bloc,
           dsend, xsend, fsend, ssend, xdrecv, xarecv, vpass, vgot):
    r = lax.axis_index("row")
    c = lax.axis_index("col")
    width = s.shape[0]
    half = width // 2
    hr = u.shape[2]
    hv = v.shape[2]
    ch = width // CHUNKS
    mine = r + c - first
    solver = (mine >= 0) & (mine < FRONTS)
    even = lax.rem(r, 2) == 0
    last = mine == FRONTS - 1
    blocks = width // LANES

    def remote(src, dst, ssem, rsem, to_row, to_col):
        return pltpu.make_async_remote_copy(
            src_ref=src, dst_ref=dst, send_sem=ssem, recv_sem=rsem,
            device_id=(to_row, to_col), device_id_type=MESH)

    def arrived(ref, sem):
        pltpu.make_async_copy(ref, ref, sem).wait()

    def span(count, body):
        def step(at, carry):
            body(at)
            return carry
        lax.fori_loop(0, count, step, 0)

    own_u = pl.ds(pl.multiple_of(c * hr, hr), hr)
    own_v = pl.ds(pl.multiple_of(r * hv, hv), hv)

    load_s = pltpu.make_async_copy(work, s, loc.at[0])
    load_u = pltpu.make_async_copy(u.at[0, 0], ubuf.at[own_u], loc.at[1])
    load_v = pltpu.make_async_copy(v.at[0, 0], vbuf.at[own_v], loc.at[2])
    load_s.start()

    @pl.when(solver)
    def _():
        for low in range(blocks):
            for high in range(low + 1, blocks):
                if low * LANES // half == high * LANES // half:
                    x, y = pl.ds(low * LANES, LANES), pl.ds(high * LANES, LANES)
                    ubuf[x, y] = jnp.zeros((LANES, LANES), F32)
                    vbuf[y, x] = jnp.zeros((LANES, LANES), F32)
        load_u.start()

    @pl.when(solver & (mine != 1))
    def _():
        load_v.start()

    barrier = pltpu.get_barrier_semaphore()

    def greet_row(at):
        @pl.when(at != r)
        def _():
            pl.semaphore_signal(barrier, inc=1, device_id=(at, c), device_id_type=MESH)

    def greet_col(at):
        @pl.when(at != c)
        def _():
            pl.semaphore_signal(barrier, inc=1, device_id=(r, at), device_id_type=MESH)

    span(rows, greet_row)
    span(cols, greet_col)
    pl.semaphore_wait(barrier, rows + cols - 2)

    def u_filled(at, body):
        reach = (at * hr + hr - 1) // LANES
        for block in range(blocks):
            @pl.when(reach == block)
            def _():
                body(pl.ds(0, (block + 1) * LANES))

    def v_filled(at, body):
        reach = at * hv // LANES
        for block in range(blocks):
            @pl.when(reach == block)
            def _():
                body(pl.ds(block * LANES, width - block * LANES))

    def factors(f, act):
        j = first + f - r

        @pl.when((j >= 0) & (j < cols) & (j != c))
        def _():
            u_filled(c, lambda part: act(remote(
                u.at[0, 0, :, part], ubuf.at[own_u, part], usend.at[f], urecv.at[c], r, j)))

        i = first + f - c

        @pl.when((f != 1) & (i >= 0) & (i < rows) & (i != r))
        def _():
            v_filled(r, lambda part: act(remote(
                v.at[0, 0, :, part], vbuf.at[own_v, part], vsend.at[f], vrecv.at[r], i, c)))

    def a_send(f, j, need, act, act_local):
        k = first + f - j

        @pl.when(need & (j != c))
        def _():
            act(remote(a.at[0, k], abuf.at[f, own_u], asend.at[f, j], arecv.at[f, c], r, j))

        @pl.when(need & (j == c))
        def _():
            act_local(pltpu.make_async_copy(a.at[0, k], abuf.at[f, own_u], aloc.at[f]))

    def b_send(f, l, need, act, act_local):
        i = first + f - l

        @pl.when(need & (i != r))
        def _():
            act(remote(b.at[l, 0], bbuf.at[f, own_v], bsend.at[f, l], brecv.at[f, r], i, c))

        @pl.when(need & (i == r))
        def _():
            act_local(pltpu.make_async_copy(b.at[l, 0], bbuf.at[f, own_v], bloc.at[f]))

    def near(f, act, act_local):
        j, i = first + f + 1 - r, first + f + 1 - c
        a_send(f, j, (j >= 0) & (j < cols) & (r >= 1), act, act_local)
        b_send(f, c - 1, (i >= 0) & (i < rows) & (c >= 1), act, act_local)

    def rest(f, act, act_local):
        def a_step(at):
            j = lax.rem(c + 1 + at, cols)
            a_send(f, j, (r + j > first + f + 1) & (first + f - j >= 0), act, act_local)

        def b_step(l):
            i = first + f - l
            b_send(f, l, (i >= 0) & (i < rows) & (c > l + 1), act, act_local)

        span(cols, a_step)
        span(cols, b_step)

    def start(copy):
        copy.start()

    def sent(copy):
        copy.wait_send()

    def nothing(copy):
        return None

    factors(0, start)
    load_s.wait()

    def send_ahead(paced):
        for f in range(1, FRONTS):
            if paced:
                factors(f - 1, sent)
                if f > 1:
                    near(f - 2, sent, nothing)
            factors(f, start)
            near(f - 1, start, start)
        if paced:
            factors(FRONTS - 1, sent)
            near(FRONTS - 2, sent, nothing)
        near(FRONTS - 1, start, start)

    @pl.when(mine != 0)
    def _():
        send_ahead(True)
        span(FRONTS, lambda f: rest(f, start, start))

    t, e = slice(0, half), slice(half, width)

    def prepare(high, low, buf, corner, scale):
        x, y = corner

        def put(slot, part, value):
            high[(slot,) + part], low[(slot,) + part] = split(value)

        def get(slot, part):
            return high[(slot,) + part], low[(slot,) + part]

        def square(slot, part):
            if part != corner:
                return product(get(slot, part), get(slot, part))
            return (product(get(slot, (x, x)), get(slot, corner))
                    + product(get(slot, corner), get(slot, (y, y))))

        parts = ((t, t), (e, e), corner)
        eye = (lax.broadcasted_iota(jnp.int32, (half, half), 0)
               == lax.broadcasted_iota(jnp.int32, (half, half), 1)).astype(F32)
        for part in parts:
            put(4, part, buf[part])
        for part in parts:
            base = buf[part]
            put(0, part, ((eye - base) if part != corner else -base) * scale)
        for part in parts:
            value = square(4, part)
            put(2, part, value)
            put(1, part, (buf[part] - value) * scale)
        for part in parts:
            put(3, part, square(2, part))

    @pl.when(solver)
    def _():
        load_u.wait()

        def u_wait(at):
            @pl.when(at != c)
            def _():
                place = pl.ds(pl.multiple_of(at * hr, hr), hr)
                u_filled(at, lambda part: arrived(ubuf.at[place, part], urecv.at[at]))

        span(cols, u_wait)
        prepare(uh, ul, ubuf, (e, t), 1.0)

    @pl.when(mine == 0)
    def _():
        send_ahead(False)

    beside = jnp.where(even, r + 1, r - 1)
    passing = solver & (mine != 1) & ((mine == 0) == even)

    def pass_v(act):
        for at, (x, y) in enumerate(((t, t), (slice(0, width), e))):
            part = vbuf.at[pl.ds(x.start, x.stop - x.start), pl.ds(y.start, y.stop - y.start)]
            act(remote(part, part, vpass.at[at], vgot.at[at], beside, c))

    @pl.when(mine == 1)
    def _():
        pass_v(lambda copy: copy.wait_recv())

    @pl.when(solver & (mine != 1))
    def _():
        load_v.wait()

        def v_wait(at):
            @pl.when(at != r)
            def _():
                place = pl.ds(pl.multiple_of(at * hv, hv), hv)
                v_filled(at, lambda part: arrived(vbuf.at[place, part], vrecv.at[at]))

        span(rows, v_wait)

        @pl.when(passing)
        def _():
            pass_v(start)

    @pl.when(solver)
    def _():
        prepare(vh, vl, vbuf, (t, e), 0.5 / jnp.broadcast_to(shift[0], (1, half)).astype(F32))

    def chunk(k):
        return pl.ds(pl.multiple_of(k * ch, ch), ch)

    def forwards(f, k, act):
        part = xd.at[f, chunk(k)]

        @pl.when(even)
        def _():
            act(remote(part, part, fsend.at[f, k, 0], xdrecv.at[f, k], r + 1, c))

            @pl.when(r + 2 < rows)
            def _():
                act(remote(part, part, fsend.at[f, k, 1], xdrecv.at[f, k], r + 2, c))

    square = cols == 4

    def sideways(f, k, act):
        if square:
            part = xa.at[f, chunk(k)]
            source = first + f - r

            @pl.when(((source == 0) & (c == 2)) | ((source == 1) & (c == 3) & (f == FRONTS - 1)))
            def _():
                act(remote(part, part, ssend.at[f, k], xarecv.at[f, k], r, 5 - c))

    def a_needed(f):
        return (mine > f) & (first + f - c >= 0)

    def b_needed(f):
        return (mine > f) & (first + f - r >= 0)

    def update(f):
        @pl.when(a_needed(f))
        def _():
            arrived(abuf.at[f, own_u], aloc.at[f])

            def a_wait(at):
                @pl.when(at != c)
                def _():
                    arrived(abuf.at[f, pl.ds(pl.multiple_of(at * hr, hr), hr)], arecv.at[f, at])

            span(cols, a_wait)

        @pl.when(b_needed(f))
        def _():
            arrived(bbuf.at[f, own_v], bloc.at[f])

            def b_wait(at):
                @pl.when(at != r)
                def _():
                    arrived(bbuf.at[f, pl.ds(pl.multiple_of(at * hv, hv), hv)], brecv.at[f, at])

            span(rows, b_wait)

        def x_wait(k):
            @pl.when(a_needed(f))
            def _():
                arrived(xd.at[f, chunk(k)], xdrecv.at[f, k])
                forwards(f, k, start)

            @pl.when(b_needed(f))
            def _():
                arrived(xa.at[f, chunk(k)], xarecv.at[f, k])
                sideways(f, k, start)

        span(CHUNKS, x_wait)

        @pl.when(a_needed(f))
        def _():
            s[...] -= dot(abuf[f], xd[f])

        @pl.when(b_needed(f))
        def _():
            s[...] -= dot(xa[f], bbuf[f])

    span(FRONTS, update)

    def spread(k, act):
        part = xs.at[chunk(k)]
        there, across = xd.at[mine, chunk(k)], xa.at[mine, chunk(k)]

        @pl.when(r + 1 < rows)
        def _():
            act(remote(part, there, dsend.at[k, 0], xdrecv.at[mine, k], r + 1, c))

        def right(at):
            relayed = (c == 0) & (at == 3) | (c == 1) & (at == 1) & last if square else at < 0

            @pl.when((c + at < cols) & jnp.logical_not(relayed))
            def _():
                act(remote(part, across, xsend.at[k, at - 1], xarecv.at[mine, k], r, c + at))

        span(cols - 1, lambda at: right(at + 1))

        @pl.when(even & (r + 2 < rows))
        def _():
            act(remote(part, there, dsend.at[k, 1], xdrecv.at[mine, k], r + 2, c))

    @pl.when(solver)
    def _():
        for part, extent in ((t, half), (e, width)):
            now = s[part, :]
            yh[0, part, :], yl[0, part, :] = split(now)

            def left(slot, stage):
                return split(product((uh[slot, part, :extent], ul[slot, part, :extent]),
                                     (yh[stage, :extent, :], yl[stage, :extent, :])))

            def right(slot, moved):
                high, low = moved
                near = product((high[:, :half], low[:, :half]),
                               (vh[slot, :half, :half], vl[slot, :half, :half]))
                far = product((high, low), (vh[slot, :, half:], vl[slot, :, half:]))
                return jnp.concatenate([near, far], axis=1)

            zero, one = left(0, 0), left(1, 0)
            now = right(0, zero) + right(1, one)
            for stage in (1, 2):
                yh[stage, part, :], yl[stage, part, :] = split(now)
                now = now + right(stage + 1, left(stage + 1, stage))
            s[part, :] = now
            xs[part, :] = now.astype(BF)
            lowest = part.start // ch

            span(CHUNKS // 2, lambda at: spread(lowest + at, start))

    @pl.when(mine == 0)
    def _():
        span(FRONTS, lambda f: rest(f, start, start))

    @pl.when(mine == 0)
    def _():
        for f in range(FRONTS):
            factors(f, sent)
        for f in range(FRONTS - 1):
            near(f, sent, nothing)

    near(FRONTS - 1, sent, nothing)
    span(FRONTS, lambda f: rest(f, sent, nothing))

    def drain(f):
        @pl.when(a_needed(f))
        def _():
            span(CHUNKS, lambda k: forwards(f, k, sent))

        @pl.when(b_needed(f))
        def _():
            span(CHUNKS, lambda k: sideways(f, k, sent))

    span(FRONTS, drain)

    @pl.when(passing)
    def _():
        pass_v(sent)

    @pl.when(solver)
    def _():
        span(CHUNKS, lambda k: spread(k, sent))


def per_device(rows, cols, work, a, b, u, v, shift):
    first = max(0, (rows + cols) // 2 - FRONTS)
    width = work.shape[0]
    tile = (width, width)
    hbm_ref = pl.BlockSpec(memory_space=pltpu.HBM)
    work, a, b, u, v = (pltpu.with_memory_space_constraint(x, pltpu.HBM) for x in (work, a, b, u, v))
    dma = pltpu.SemaphoreType.DMA
    stack = [pltpu.VMEM((FRONTS,) + tile, BF)]
    return pl.pallas_call(
        functools.partial(kernel, rows, cols, first),
        out_shape=pltpu.VMEM(work.shape, work.dtype),
        in_specs=[hbm_ref] * 5 + [pl.BlockSpec(memory_space=pltpu.SMEM)],
        out_specs=pl.BlockSpec(memory_space=pltpu.VMEM),
        scratch_shapes=[pltpu.VMEM(tile, F32)] * 2 + [pltpu.VMEM((5,) + tile, BF)] * 4
        + [pltpu.VMEM((3,) + tile, BF)] * 2
        + [pltpu.VMEM(tile, BF)] + stack * 4
        + [dma((3,)), dma((FRONTS,)), dma((cols,)), dma((FRONTS,)), dma((rows,)),
           dma((FRONTS, cols)), dma((FRONTS, cols)), dma((FRONTS,)),
           dma((FRONTS, cols)), dma((FRONTS, rows)), dma((FRONTS,)),
           dma((CHUNKS, 2)), dma((CHUNKS, cols - 1)), dma((FRONTS, CHUNKS, 2)),
           dma((FRONTS, CHUNKS)), dma((FRONTS, CHUNKS)), dma((FRONTS, CHUNKS)), dma((2,)), dma((2,))],
        compiler_params=pltpu.CompilerParams(
            collective_id=0, has_side_effects=True, vmem_limit_bytes=48 * 1024 * 1024),
    )(work, a, b, u, v, shift)


def solution(mesh):
    placed = (
        P("row", "col"),
        P("row", None, "col", None),
        P(None, "col", "row", None),
        P("row", None, "col", None),
        P("col", None, "row", None),
        P(),
    )
    return jax.shard_map(
        functools.partial(per_device, mesh.shape["row"], mesh.shape["col"]),
        mesh=mesh, in_specs=placed, out_specs=P("row", "col"), check_vma=False
    )
```

```python
import functools
import jax
import jax.numpy as jnp
from jax import lax
from jax.experimental import pallas as pl
from jax.experimental.pallas import tpu as pltpu
from jax.sharding import PartitionSpec as P

FRONTS = 3
CHUNKS = 8
LANES = 128
MESH = pl.DeviceIdType.MESH
BF = jnp.bfloat16
F32 = jnp.float32


def dot(left, right):
    return jnp.dot(left, right, preferred_element_type=F32)


def split(value):
    high = value.astype(BF)
    return high, (value - high.astype(F32)).astype(BF)


def lay_left(parts):
    high, low = parts
    return [high, high, low]


def lay_right(parts):
    high, low = parts
    return [high, low, high]


def product(lefts, rights):
    left = jnp.concatenate(sum(map(lay_left, lefts), []), axis=1)
    return dot(left, jnp.concatenate(sum(map(lay_right, rights), []), axis=0))


def kernel(rows, cols, first, work, a, b, u, v, shift, s,
           ubuf, vbuf, utop, ulow, vnear, vfar, y, xs, abuf, bbuf, xd, xa,
           loc, usend, urecv, vsend, vrecv, asend, arecv, aloc, bsend, brecv, bloc,
           dsend, xsend, fsend, ssend, xdrecv, xarecv, vpass, vgot):
    r = lax.axis_index("row")
    c = lax.axis_index("col")
    width = s.shape[0]
    half = width // 2
    hr = u.shape[2]
    hv = v.shape[2]
    ch = width // CHUNKS
    mine = r + c - first
    solver = (mine >= 0) & (mine < FRONTS)
    even = lax.rem(r, 2) == 0
    last = mine == FRONTS - 1
    blocks = width // LANES

    def remote(src, dst, ssem, rsem, to_row, to_col):
        return pltpu.make_async_remote_copy(
            src_ref=src, dst_ref=dst, send_sem=ssem, recv_sem=rsem,
            device_id=(to_row, to_col), device_id_type=MESH)

    def arrived(ref, sem):
        pltpu.make_async_copy(ref, ref, sem).wait()

    def span(count, body):
        def step(at, carry):
            body(at)
            return carry
        lax.fori_loop(0, count, step, 0)

    own_u = pl.ds(pl.multiple_of(c * hr, hr), hr)
    own_v = pl.ds(pl.multiple_of(r * hv, hv), hv)

    load_s = pltpu.make_async_copy(work, s, loc.at[0])
    load_u = pltpu.make_async_copy(u.at[0, 0], ubuf.at[own_u], loc.at[1])
    load_v = pltpu.make_async_copy(v.at[0, 0], vbuf.at[own_v], loc.at[2])
    load_s.start()

    @pl.when(solver)
    def _():
        for low in range(blocks):
            for high in range(low + 1, blocks):
                if low * LANES // half == high * LANES // half:
                    x, y = pl.ds(low * LANES, LANES), pl.ds(high * LANES, LANES)
                    ubuf[x, y] = jnp.zeros((LANES, LANES), F32)
                    vbuf[y, x] = jnp.zeros((LANES, LANES), F32)
        load_u.start()

    @pl.when(solver & (mine != 1))
    def _():
        load_v.start()

    barrier = pltpu.get_barrier_semaphore()

    def greet_row(at):
        @pl.when(at != r)
        def _():
            pl.semaphore_signal(barrier, inc=1, device_id=(at, c), device_id_type=MESH)

    def greet_col(at):
        @pl.when(at != c)
        def _():
            pl.semaphore_signal(barrier, inc=1, device_id=(r, at), device_id_type=MESH)

    span(rows, greet_row)
    span(cols, greet_col)
    pl.semaphore_wait(barrier, rows + cols - 2)

    def u_filled(at, body):
        reach = (at * hr + hr - 1) // LANES
        for block in range(blocks):
            @pl.when(reach == block)
            def _():
                body(pl.ds(0, (block + 1) * LANES))

    def v_filled(at, body):
        reach = at * hv // LANES
        for block in range(blocks):
            @pl.when(reach == block)
            def _():
                body(pl.ds(block * LANES, width - block * LANES))

    def factors(f, act):
        j = first + f - r

        @pl.when((j >= 0) & (j < cols) & (j != c))
        def _():
            u_filled(c, lambda part: act(remote(
                u.at[0, 0, :, part], ubuf.at[own_u, part], usend.at[f], urecv.at[c], r, j)))

        i = first + f - c

        @pl.when((f != 1) & (i >= 0) & (i < rows) & (i != r))
        def _():
            v_filled(r, lambda part: act(remote(
                v.at[0, 0, :, part], vbuf.at[own_v, part], vsend.at[f], vrecv.at[r], i, c)))

    def a_send(f, j, need, act, act_local):
        k = first + f - j

        @pl.when(need & (j != c))
        def _():
            act(remote(a.at[0, k], abuf.at[f, own_u], asend.at[f, j], arecv.at[f, c], r, j))

        @pl.when(need & (j == c))
        def _():
            act_local(pltpu.make_async_copy(a.at[0, k], abuf.at[f, own_u], aloc.at[f]))

    def b_send(f, l, need, act, act_local):
        i = first + f - l

        @pl.when(need & (i != r))
        def _():
            act(remote(b.at[l, 0], bbuf.at[f, own_v], bsend.at[f, l], brecv.at[f, r], i, c))

        @pl.when(need & (i == r))
        def _():
            act_local(pltpu.make_async_copy(b.at[l, 0], bbuf.at[f, own_v], bloc.at[f]))

    def near(f, act, act_local):
        j, i = first + f + 1 - r, first + f + 1 - c
        a_send(f, j, (j >= 0) & (j < cols) & (r >= 1), act, act_local)
        b_send(f, c - 1, (i >= 0) & (i < rows) & (c >= 1), act, act_local)

    def rest(f, act, act_local):
        def a_step(at):
            j = lax.rem(c + 1 + at, cols)
            a_send(f, j, (r + j > first + f + 1) & (first + f - j >= 0), act, act_local)

        def b_step(l):
            i = first + f - l
            b_send(f, l, (i >= 0) & (i < rows) & (c > l + 1), act, act_local)

        span(cols, a_step)
        span(cols, b_step)

    def start(copy):
        copy.start()

    def sent(copy):
        copy.wait_send()

    def nothing(copy):
        return None

    factors(0, start)
    load_s.wait()

    def send_ahead(paced):
        for f in range(1, FRONTS):
            if paced:
                factors(f - 1, sent)
                if f > 1:
                    near(f - 2, sent, nothing)
            factors(f, start)
            near(f - 1, start, start)
        if paced:
            factors(FRONTS - 1, sent)
            near(FRONTS - 2, sent, nothing)
        near(FRONTS - 1, start, start)

    @pl.when(mine != 0)
    def _():
        send_ahead(True)
        span(FRONTS, lambda f: rest(f, start, start))

    t, e = slice(0, half), slice(half, width)

    def prepare(buf, corner, scale, keep):
        x, z = corner
        parts = ((t, t), (e, e), corner)
        eye = (lax.broadcasted_iota(jnp.int32, (half, half), 0)
               == lax.broadcasted_iota(jnp.int32, (half, half), 1)).astype(F32)

        def squares(values):
            both = [split(value) for value in values]
            out = [product([both[at]], [both[at]]) for at in range(2)]
            first_at, second_at = (0, 1) if x == t else (1, 0)
            out.append(product([both[first_at], both[2]], [both[2], both[second_at]]))
            return out, both

        base = [buf[p, q] for p, q in parts]
        second, _ = squares(base)
        for at, part in enumerate(parts):
            keep(0, at, split(((eye - base[at]) if at < 2 else -base[at]) * scale))
            keep(1, at, split((base[at] - second[at]) * scale))
        fourth, both = squares(second)
        for at, part in enumerate(parts):
            keep(2, at, both[at])
            keep(3, at, split(fourth[at]))

    def keep_u(slot, at, parts):
        value = jnp.concatenate(lay_left(parts), axis=1)
        if at == 0:
            utop[slot] = value
        else:
            place = 3 * half * (2 - at)
            ulow[slot, :, place:place + 3 * half] = value

    def keep_v(slot, at, parts):
        value = jnp.concatenate(lay_right(parts), axis=0)
        if at == 0:
            vnear[slot * 3 * half:(slot + 1) * 3 * half, :] = value
        else:
            place = (2 * slot + 2 - at) * 3 * half
            vfar[place:place + 3 * half, :] = value

    @pl.when(solver)
    def _():
        load_u.wait()

        def u_wait(at):
            @pl.when(at != c)
            def _():
                place = pl.ds(pl.multiple_of(at * hr, hr), hr)
                u_filled(at, lambda part: arrived(ubuf.at[place, part], urecv.at[at]))

        span(cols, u_wait)
        prepare(ubuf, (e, t), 1.0, keep_u)

    @pl.when(mine == 0)
    def _():
        send_ahead(False)

    beside = jnp.where(even, r + 1, r - 1)
    passing = solver & (mine != 1) & ((mine == 0) == even)

    def pass_v(act):
        for at, (x, y) in enumerate(((t, t), (slice(0, width), e))):
            part = vbuf.at[pl.ds(x.start, x.stop - x.start), pl.ds(y.start, y.stop - y.start)]
            act(remote(part, part, vpass.at[at], vgot.at[at], beside, c))

    @pl.when(mine == 1)
    def _():
        pass_v(lambda copy: copy.wait_recv())

    @pl.when(solver & (mine != 1))
    def _():
        load_v.wait()

        def v_wait(at):
            @pl.when(at != r)
            def _():
                place = pl.ds(pl.multiple_of(at * hv, hv), hv)
                v_filled(at, lambda part: arrived(vbuf.at[place, part], vrecv.at[at]))

        span(rows, v_wait)

        @pl.when(passing)
        def _():
            pass_v(start)

    @pl.when(solver)
    def _():
        prepare(vbuf, (t, e), 0.5 / jnp.broadcast_to(shift[0], (1, half)).astype(F32), keep_v)

    def chunk(k):
        return pl.ds(pl.multiple_of(k * ch, ch), ch)

    def forwards(f, k, act):
        part = xd.at[f, chunk(k)]

        @pl.when(even)
        def _():
            act(remote(part, part, fsend.at[f, k, 0], xdrecv.at[f, k], r + 1, c))

            @pl.when(r + 2 < rows)
            def _():
                act(remote(part, part, fsend.at[f, k, 1], xdrecv.at[f, k], r + 2, c))

    square = cols == 4

    def relays(f):
        source = first + f - r
        if not square:
            return source < 0
        return ((source == 0) & (c == 2)) | ((source == 1) & (c == 3) & (f == FRONTS - 1))

    def sideways(f, k, act):
        if square:
            part = xa.at[f, chunk(k)]

            @pl.when(relays(f))
            def _():
                act(remote(part, part, ssend.at[f, k], xarecv.at[f, k], r, 5 - c))

    def a_needed(f):
        return (mine > f) & (first + f - c >= 0)

    def b_needed(f):
        return (mine > f) & (first + f - r >= 0)

    def update(f):
        @pl.when(a_needed(f))
        def _():
            arrived(abuf.at[f, own_u], aloc.at[f])

            def a_wait(at):
                @pl.when(at != c)
                def _():
                    arrived(abuf.at[f, pl.ds(pl.multiple_of(at * hr, hr), hr)], arecv.at[f, at])

            span(cols, a_wait)

        @pl.when(b_needed(f))
        def _():
            arrived(bbuf.at[f, own_v], bloc.at[f])

            def b_wait(at):
                @pl.when(at != r)
                def _():
                    arrived(bbuf.at[f, pl.ds(pl.multiple_of(at * hv, hv), hv)], brecv.at[f, at])

            span(rows, b_wait)

        def d_wait(k):
            arrived(xd.at[f, chunk(k)], xdrecv.at[f, k])
            forwards(f, k, start)

        def x_wait(k):
            arrived(xa.at[f, chunk(k)], xarecv.at[f, k])
            sideways(f, k, start)

        relay = b_needed(f) & relays(f)

        @pl.when(relay)
        def _():
            span(CHUNKS, x_wait)

        @pl.when(a_needed(f))
        def _():
            span(CHUNKS, d_wait)
            s[...] -= dot(abuf[f], xd[f])

        @pl.when(b_needed(f) & jnp.logical_not(relay))
        def _():
            span(CHUNKS, x_wait)

        @pl.when(b_needed(f))
        def _():
            s[...] -= dot(xa[f], bbuf[f])

    span(FRONTS, update)

    def spread(k, act):
        part = xs.at[chunk(k)]
        there, across = xd.at[mine, chunk(k)], xa.at[mine, chunk(k)]

        @pl.when(r + 1 < rows)
        def _():
            act(remote(part, there, dsend.at[k, 0], xdrecv.at[mine, k], r + 1, c))

        def right(at):
            relayed = (c == 0) & (at == 3) | (c == 1) & (at == 1) & last if square else at < 0

            @pl.when((c + at < cols) & jnp.logical_not(relayed))
            def _():
                act(remote(part, across, xsend.at[k, at - 1], xarecv.at[mine, k], r, c + at))

        span(cols - 1, lambda at: right(at + 1))

        @pl.when(even & (r + 2 < rows))
        def _():
            act(remote(part, there, dsend.at[k, 1], xdrecv.at[mine, k], r + 2, c))

    @pl.when(solver)
    def _():
        def put(stage, at, value):
            y[stage, at * 3 * half:(at + 1) * 3 * half, :] = jnp.concatenate(
                lay_right(split(value)), axis=0)

        for at, part in enumerate((t, e)):
            put(0, at, s[part, :])

            def left(slot, stage):
                if at == 0:
                    moved = dot(utop[slot], y[stage, :3 * half, :])
                else:
                    moved = dot(ulow[slot], y[stage])
                high, low = split(moved)
                return lay_left((high[:, :half], low[:, :half])), lay_left((high[:, half:], low[:, half:]))

            def right(slot, moved):
                count = len(moved)
                near_part = jnp.concatenate(sum((m[0] for m in moved), []), axis=1)
                far_part = jnp.concatenate(sum((m[0] + m[1] for m in moved), []), axis=1)
                left_half = dot(near_part, vnear[slot * 3 * half:(slot + count) * 3 * half, :])
                right_half = dot(far_part, vfar[slot * 6 * half:(slot + count) * 6 * half, :])
                return jnp.concatenate([left_half, right_half], axis=1)

            now = right(0, [left(0, 0), left(1, 0)])
            for stage in (1, 2):
                put(stage, at, now)
                now = now + right(stage + 1, [left(stage + 1, stage)])
            s[part, :] = now
            xs[part, :] = now.astype(BF)
            lowest = part.start // ch

            span(CHUNKS // 2, lambda at: spread(lowest + at, start))

    @pl.when(mine == 0)
    def _():
        span(FRONTS, lambda f: rest(f, start, start))

    @pl.when(mine == 0)
    def _():
        for f in range(FRONTS):
            factors(f, sent)
        for f in range(FRONTS - 1):
            near(f, sent, nothing)

    near(FRONTS - 1, sent, nothing)
    span(FRONTS, lambda f: rest(f, sent, nothing))

    def drain(f):
        @pl.when(a_needed(f))
        def _():
            span(CHUNKS, lambda k: forwards(f, k, sent))

        @pl.when(b_needed(f))
        def _():
            span(CHUNKS, lambda k: sideways(f, k, sent))

    span(FRONTS, drain)

    @pl.when(passing)
    def _():
        pass_v(sent)

    @pl.when(solver)
    def _():
        span(CHUNKS, lambda k: spread(k, sent))


def per_device(rows, cols, work, a, b, u, v, shift):
    first = max(0, (rows + cols) // 2 - FRONTS)
    width = work.shape[0]
    tile, half = (width, width), width // 2
    hbm_ref = pl.BlockSpec(memory_space=pltpu.HBM)
    work, a, b, u, v = (pltpu.with_memory_space_constraint(x, pltpu.HBM) for x in (work, a, b, u, v))
    dma = pltpu.SemaphoreType.DMA
    stack = [pltpu.VMEM((FRONTS,) + tile, BF)]
    return pl.pallas_call(
        functools.partial(kernel, rows, cols, first),
        out_shape=pltpu.VMEM(work.shape, work.dtype),
        in_specs=[hbm_ref] * 5 + [pl.BlockSpec(memory_space=pltpu.SMEM)],
        out_specs=pl.BlockSpec(memory_space=pltpu.VMEM),
        scratch_shapes=[pltpu.VMEM(tile, F32)] * 2 + [
            pltpu.VMEM((4, half, 3 * half), BF), pltpu.VMEM((4, half, 6 * half), BF),
            pltpu.VMEM((12 * half, half), BF), pltpu.VMEM((24 * half, half), BF),
            pltpu.VMEM((3, 6 * half, width), BF)]
        + [pltpu.VMEM(tile, BF)] + stack * 4
        + [dma((3,)), dma((FRONTS,)), dma((cols,)), dma((FRONTS,)), dma((rows,)),
           dma((FRONTS, cols)), dma((FRONTS, cols)), dma((FRONTS,)),
           dma((FRONTS, cols)), dma((FRONTS, rows)), dma((FRONTS,)),
           dma((CHUNKS, 2)), dma((CHUNKS, cols - 1)), dma((FRONTS, CHUNKS, 2)),
           dma((FRONTS, CHUNKS)), dma((FRONTS, CHUNKS)), dma((FRONTS, CHUNKS)), dma((2,)), dma((2,))],
        compiler_params=pltpu.CompilerParams(
            collective_id=0, has_side_effects=True, vmem_limit_bytes=48 * 1024 * 1024),
    )(work, a, b, u, v, shift)


def solution(mesh):
    placed = (
        P("row", "col"),
        P("row", None, "col", None),
        P(None, "col", "row", None),
        P("row", None, "col", None),
        P("col", None, "row", None),
        P(),
    )
    return jax.shard_map(
        functools.partial(per_device, mesh.shape["row"], mesh.shape["col"]),
        mesh=mesh, in_specs=placed, out_specs=P("row", "col"), check_vma=False
    )
```

```python
import functools
import jax
import jax.numpy as jnp
from jax import lax
from jax.experimental import pallas as pl
from jax.experimental.pallas import tpu as pltpu
from jax.sharding import PartitionSpec as P

FRONTS = 3
CHUNKS = 8
LANES = 128
MESH = pl.DeviceIdType.MESH
BF = jnp.bfloat16
F32 = jnp.float32


def dot(left, right):
    return jnp.dot(left, right, preferred_element_type=F32)


def split(value):
    high = value.astype(BF)
    return high, (value - high.astype(F32)).astype(BF)


def lay_left(parts):
    high, low = parts
    return [high, high, low]


def lay_right(parts):
    high, low = parts
    return [high, low, high]


def product(lefts, rights):
    left = jnp.concatenate(sum(map(lay_left, lefts), []), axis=1)
    return dot(left, jnp.concatenate(sum(map(lay_right, rights), []), axis=0))


def kernel(rows, cols, first, work, a, b, u, v, shift, s,
           ubuf, vbuf, utop, ulow, vnear, vfar, y, begun, xs, abuf, bbuf, xd, xa,
           loc, usend, urecv, vsend, vrecv, asend, arecv, aloc, bsend, brecv, bloc,
           dsend, xsend, fsend, ssend, xdrecv, xarecv, vpass, vgot):
    r = lax.axis_index("row")
    c = lax.axis_index("col")
    width = s.shape[0]
    half = width // 2
    hr = u.shape[2]
    hv = v.shape[2]
    ch = width // CHUNKS
    mine = r + c - first
    solver = (mine >= 0) & (mine < FRONTS)
    even = lax.rem(r, 2) == 0
    last = mine == FRONTS - 1
    blocks = width // LANES

    def remote(src, dst, ssem, rsem, to_row, to_col):
        return pltpu.make_async_remote_copy(
            src_ref=src, dst_ref=dst, send_sem=ssem, recv_sem=rsem,
            device_id=(to_row, to_col), device_id_type=MESH)

    def arrived(ref, sem):
        pltpu.make_async_copy(ref, ref, sem).wait()

    def span(count, body):
        def step(at, carry):
            body(at)
            return carry
        lax.fori_loop(0, count, step, 0)

    own_u = pl.ds(pl.multiple_of(c * hr, hr), hr)
    own_v = pl.ds(pl.multiple_of(r * hv, hv), hv)

    load_s = pltpu.make_async_copy(work, s, loc.at[0])
    load_u = pltpu.make_async_copy(u.at[0, 0], ubuf.at[own_u], loc.at[1])
    load_v = pltpu.make_async_copy(v.at[0, 0], vbuf.at[own_v], loc.at[2])
    load_s.start()

    @pl.when(solver)
    def _():
        for low in range(blocks):
            for high in range(low + 1, blocks):
                if low * LANES // half == high * LANES // half:
                    x, y = pl.ds(low * LANES, LANES), pl.ds(high * LANES, LANES)
                    ubuf[x, y] = jnp.zeros((LANES, LANES), F32)
                    vbuf[y, x] = jnp.zeros((LANES, LANES), F32)
        load_u.start()

    @pl.when(solver & (mine != 1))
    def _():
        load_v.start()

    barrier = pltpu.get_barrier_semaphore()

    def greet_row(at):
        @pl.when(at != r)
        def _():
            pl.semaphore_signal(barrier, inc=1, device_id=(at, c), device_id_type=MESH)

    def greet_col(at):
        @pl.when(at != c)
        def _():
            pl.semaphore_signal(barrier, inc=1, device_id=(r, at), device_id_type=MESH)

    span(rows, greet_row)
    span(cols, greet_col)
    pl.semaphore_wait(barrier, rows + cols - 2)

    def u_filled(at, body):
        reach = (at * hr + hr - 1) // LANES
        for block in range(blocks):
            @pl.when(reach == block)
            def _():
                body(pl.ds(0, (block + 1) * LANES))

    def v_filled(at, body):
        reach = at * hv // LANES
        for block in range(blocks):
            @pl.when(reach == block)
            def _():
                body(pl.ds(block * LANES, width - block * LANES))

    def factors(f, act):
        j = first + f - r

        @pl.when((j >= 0) & (j < cols) & (j != c))
        def _():
            u_filled(c, lambda part: act(remote(
                u.at[0, 0, :, part], ubuf.at[own_u, part], usend.at[f], urecv.at[c], r, j)))

        i = first + f - c

        @pl.when((f != 1) & (i >= 0) & (i < rows) & (i != r))
        def _():
            v_filled(r, lambda part: act(remote(
                v.at[0, 0, :, part], vbuf.at[own_v, part], vsend.at[f], vrecv.at[r], i, c)))

    def a_send(f, j, need, act, act_local):
        k = first + f - j

        @pl.when(need & (j != c))
        def _():
            act(remote(a.at[0, k], abuf.at[f, own_u], asend.at[f, j], arecv.at[f, c], r, j))

        @pl.when(need & (j == c))
        def _():
            act_local(pltpu.make_async_copy(a.at[0, k], abuf.at[f, own_u], aloc.at[f]))

    def b_send(f, l, need, act, act_local):
        i = first + f - l

        @pl.when(need & (i != r))
        def _():
            act(remote(b.at[l, 0], bbuf.at[f, own_v], bsend.at[f, l], brecv.at[f, r], i, c))

        @pl.when(need & (i == r))
        def _():
            act_local(pltpu.make_async_copy(b.at[l, 0], bbuf.at[f, own_v], bloc.at[f]))

    def near(f, act, act_local):
        j, i = first + f + 1 - r, first + f + 1 - c
        a_send(f, j, (j >= 0) & (j < cols) & (r >= 1), act, act_local)
        b_send(f, c - 1, (i >= 0) & (i < rows) & (c >= 1), act, act_local)

    def rest(f, act, act_local):
        def a_step(at):
            j = lax.rem(c + 1 + at, cols)
            a_send(f, j, (r + j > first + f + 1) & (first + f - j >= 0), act, act_local)

        def b_step(l):
            i = first + f - l
            b_send(f, l, (i >= 0) & (i < rows) & (c > l + 1), act, act_local)

        span(cols, a_step)
        span(cols, b_step)

    def start(copy):
        copy.start()

    def sent(copy):
        copy.wait_send()

    def nothing(copy):
        return None

    factors(0, start)
    load_s.wait()

    def send_ahead(paced):
        for f in range(1, FRONTS):
            if paced:
                factors(f - 1, sent)
                if f > 1:
                    near(f - 2, sent, nothing)
            factors(f, start)
            near(f - 1, start, start)
        if paced:
            factors(FRONTS - 1, sent)
            near(FRONTS - 2, sent, nothing)
        near(FRONTS - 1, start, start)

    @pl.when(mine != 0)
    def _():
        send_ahead(True)
        span(FRONTS, lambda f: rest(f, start, start))

    t, e = slice(0, half), slice(half, width)

    def prepare(buf, corner, scale, keep):
        x, z = corner
        parts = ((t, t), (e, e), corner)
        eye = (lax.broadcasted_iota(jnp.int32, (half, half), 0)
               == lax.broadcasted_iota(jnp.int32, (half, half), 1)).astype(F32)

        def squares(values):
            both = [split(value) for value in values]
            out = [product([both[at]], [both[at]]) for at in range(2)]
            first_at, second_at = (0, 1) if x == t else (1, 0)
            out.append(product([both[first_at], both[2]], [both[2], both[second_at]]))
            return out, both

        base = [buf[p, q] for p, q in parts]
        second, _ = squares(base)
        for at, part in enumerate(parts):
            keep(0, at, split(((eye - base[at]) if at < 2 else -base[at]) * scale))
            keep(1, at, split((base[at] - second[at]) * scale))
        fourth, both = squares(second)
        for at, part in enumerate(parts):
            keep(2, at, both[at])
            keep(3, at, split(fourth[at]))

    def keep_u(slot, at, parts):
        value = jnp.concatenate(lay_left(parts), axis=1)
        if at == 0:
            utop[slot] = value
        else:
            place = 3 * half * (2 - at)
            ulow[slot, :, place:place + 3 * half] = value

    def keep_v(slot, at, parts):
        value = jnp.concatenate(lay_right(parts), axis=0)
        if at == 0:
            vnear[slot * 3 * half:(slot + 1) * 3 * half, :] = value
        else:
            place = (2 * slot + 2 - at) * 3 * half
            vfar[place:place + 3 * half, :] = value

    @pl.when(solver)
    def _():
        load_u.wait()

        def u_wait(at):
            @pl.when(at != c)
            def _():
                place = pl.ds(pl.multiple_of(at * hr, hr), hr)
                u_filled(at, lambda part: arrived(ubuf.at[place, part], urecv.at[at]))

        span(cols, u_wait)
        prepare(ubuf, (e, t), 1.0, keep_u)

    def put(stage, at, value):
        y[stage, at * 3 * half:(at + 1) * 3 * half, :] = jnp.concatenate(
            lay_right(split(value)), axis=0)

    def left(at, slot, stage):
        if at == 0:
            moved = dot(utop[slot], y[stage, :3 * half, :])
        else:
            moved = dot(ulow[slot], y[stage])
        high, low = split(moved)
        return jnp.concatenate(lay_left((high[:, :half], low[:, :half]))
                               + lay_left((high[:, half:], low[:, half:])), axis=1)

    def begin(at):
        put(0, at, s[(t, e)[at], :])
        begun[at, :, :6 * half] = left(at, 0, 0)
        begun[at, :, 6 * half:] = left(at, 1, 0)

    @pl.when(mine == 0)
    def _():
        send_ahead(False)
        begin(0)
        begin(1)

    beside = jnp.where(even, r + 1, r - 1)
    passing = solver & (mine != 1) & ((mine == 0) == even)

    def pass_v(act):
        for at, (x, y) in enumerate(((t, t), (slice(0, width), e))):
            part = vbuf.at[pl.ds(x.start, x.stop - x.start), pl.ds(y.start, y.stop - y.start)]
            act(remote(part, part, vpass.at[at], vgot.at[at], beside, c))

    @pl.when(mine == 1)
    def _():
        pass_v(lambda copy: copy.wait_recv())

    @pl.when(solver & (mine != 1))
    def _():
        load_v.wait()

        def v_wait(at):
            @pl.when(at != r)
            def _():
                place = pl.ds(pl.multiple_of(at * hv, hv), hv)
                v_filled(at, lambda part: arrived(vbuf.at[place, part], vrecv.at[at]))

        span(rows, v_wait)

        @pl.when(passing)
        def _():
            pass_v(start)

    @pl.when(solver)
    def _():
        prepare(vbuf, (t, e), 0.5 / jnp.broadcast_to(shift[0], (1, half)).astype(F32), keep_v)

    def chunk(k):
        return pl.ds(pl.multiple_of(k * ch, ch), ch)

    def forwards(f, k, act):
        part = xd.at[f, chunk(k)]

        @pl.when(even)
        def _():
            act(remote(part, part, fsend.at[f, k, 0], xdrecv.at[f, k], r + 1, c))

            @pl.when(r + 2 < rows)
            def _():
                act(remote(part, part, fsend.at[f, k, 1], xdrecv.at[f, k], r + 2, c))

    square = cols == 4

    def relays(f):
        source = first + f - r
        if not square:
            return source < 0
        final = f == FRONTS - 1
        onward = (c == 2) & ((source == 0) | ((source == 1) & jnp.logical_not(final)))
        return onward | ((c == 3) & (source == 1) & final)

    def sideways(f, k, act):
        if square:
            part = xa.at[f, chunk(k)]

            @pl.when(relays(f))
            def _():
                act(remote(part, part, ssend.at[f, k], xarecv.at[f, k], r, 5 - c))

    def a_needed(f):
        return (mine > f) & (first + f - c >= 0)

    def b_needed(f):
        return (mine > f) & (first + f - r >= 0)

    def update(f):
        @pl.when(a_needed(f))
        def _():
            arrived(abuf.at[f, own_u], aloc.at[f])

            def a_wait(at):
                @pl.when(at != c)
                def _():
                    arrived(abuf.at[f, pl.ds(pl.multiple_of(at * hr, hr), hr)], arecv.at[f, at])

            span(cols, a_wait)

        @pl.when(b_needed(f))
        def _():
            arrived(bbuf.at[f, own_v], bloc.at[f])

            def b_wait(at):
                @pl.when(at != r)
                def _():
                    arrived(bbuf.at[f, pl.ds(pl.multiple_of(at * hv, hv), hv)], brecv.at[f, at])

            span(rows, b_wait)

        def d_wait(k):
            arrived(xd.at[f, chunk(k)], xdrecv.at[f, k])
            forwards(f, k, start)

        def x_wait(k):
            arrived(xa.at[f, chunk(k)], xarecv.at[f, k])
            sideways(f, k, start)

        relay = b_needed(f) & relays(f)

        @pl.when(relay)
        def _():
            span(CHUNKS, x_wait)
            s[...] -= dot(xa[f], bbuf[f])

        @pl.when(a_needed(f))
        def _():
            span(CHUNKS, d_wait)
            s[...] -= dot(abuf[f], xd[f])

        @pl.when(b_needed(f) & jnp.logical_not(relay))
        def _():
            span(CHUNKS, x_wait)
            s[...] -= dot(xa[f], bbuf[f])

    span(FRONTS, update)

    held = (c == 0) & (mine == 0) & square

    def spread_held(k, act):
        if square:
            act(remote(xs.at[chunk(k)], xa.at[mine, chunk(k)], xsend.at[k, 1], xarecv.at[mine, k], r, 2))

    def spread(k, act):
        part = xs.at[chunk(k)]
        there, across = xd.at[mine, chunk(k)], xa.at[mine, chunk(k)]

        @pl.when(r + 1 < rows)
        def _():
            act(remote(part, there, dsend.at[k, 0], xdrecv.at[mine, k], r + 1, c))

        def right(at):
            relayed = at < 0
            if square:
                relayed = ((c == 0) & (at == 3)) | ((c == 1) & (at == jnp.where(last, 1, 2))) | (held & (at == 2))

            @pl.when((c + at < cols) & jnp.logical_not(relayed))
            def _():
                act(remote(part, across, xsend.at[k, at - 1], xarecv.at[mine, k], r, c + at))

        span(cols - 1, lambda at: right(at + 1))

        @pl.when(even & (r + 2 < rows))
        def _():
            act(remote(part, there, dsend.at[k, 1], xdrecv.at[mine, k], r + 2, c))

    @pl.when(solver)
    def _():
        for at, part in enumerate((t, e)):
            @pl.when(mine != 0)
            def _():
                begin(at)

            def right(slot, count, moved):
                left_half = dot(jnp.concatenate([m[:, :3 * half] for m in moved], axis=1),
                                vnear[slot * 3 * half:(slot + count) * 3 * half, :])
                right_half = dot(jnp.concatenate(moved, axis=1) if count > 1 else moved[0],
                                 vfar[slot * 6 * half:(slot + count) * 6 * half, :])
                return jnp.concatenate([left_half, right_half], axis=1)

            now = right(0, 2, [begun[at, :, :6 * half], begun[at, :, 6 * half:]])
            for stage in (1, 2):
                put(stage, at, now)
                now = now + right(stage + 1, 1, [left(at, stage + 1, stage)])
            s[part, :] = now
            xs[part, :] = now.astype(BF)
            lowest = part.start // ch

            span(CHUNKS // 2, lambda at: spread(lowest + at, start))

    @pl.when(mine == 0)
    def _():
        span(FRONTS, lambda f: rest(f, start, start))

    @pl.when(held)
    def _():
        span(CHUNKS, lambda k: spread(k, sent))
        span(CHUNKS, lambda k: spread_held(k, start))

    @pl.when(mine == 0)
    def _():
        for f in range(FRONTS):
            factors(f, sent)
        for f in range(FRONTS - 1):
            near(f, sent, nothing)

    near(FRONTS - 1, sent, nothing)
    span(FRONTS, lambda f: rest(f, sent, nothing))

    def drain(f):
        @pl.when(a_needed(f))
        def _():
            span(CHUNKS, lambda k: forwards(f, k, sent))

        @pl.when(b_needed(f))
        def _():
            span(CHUNKS, lambda k: sideways(f, k, sent))

    span(FRONTS, drain)

    @pl.when(passing)
    def _():
        pass_v(sent)

    @pl.when(held)
    def _():
        span(CHUNKS, lambda k: spread_held(k, sent))

    @pl.when(solver & jnp.logical_not(held))
    def _():
        span(CHUNKS, lambda k: spread(k, sent))


def per_device(rows, cols, work, a, b, u, v, shift):
    first = max(0, (rows + cols) // 2 - FRONTS)
    width = work.shape[0]
    tile, half = (width, width), width // 2
    hbm_ref = pl.BlockSpec(memory_space=pltpu.HBM)
    work, a, b, u, v = (pltpu.with_memory_space_constraint(x, pltpu.HBM) for x in (work, a, b, u, v))
    dma = pltpu.SemaphoreType.DMA
    stack = [pltpu.VMEM((FRONTS,) + tile, BF)]
    return pl.pallas_call(
        functools.partial(kernel, rows, cols, first),
        out_shape=pltpu.VMEM(work.shape, work.dtype),
        in_specs=[hbm_ref] * 5 + [pl.BlockSpec(memory_space=pltpu.SMEM)],
        out_specs=pl.BlockSpec(memory_space=pltpu.VMEM),
        scratch_shapes=[pltpu.VMEM(tile, F32)] * 2 + [
            pltpu.VMEM((4, half, 3 * half), BF), pltpu.VMEM((4, half, 6 * half), BF),
            pltpu.VMEM((12 * half, half), BF), pltpu.VMEM((24 * half, half), BF),
            pltpu.VMEM((3, 6 * half, width), BF), pltpu.VMEM((2, half, 12 * half), BF)]
        + [pltpu.VMEM(tile, BF)] + stack * 4
        + [dma((3,)), dma((FRONTS,)), dma((cols,)), dma((FRONTS,)), dma((rows,)),
           dma((FRONTS, cols)), dma((FRONTS, cols)), dma((FRONTS,)),
           dma((FRONTS, cols)), dma((FRONTS, rows)), dma((FRONTS,)),
           dma((CHUNKS, 2)), dma((CHUNKS, cols - 1)), dma((FRONTS, CHUNKS, 2)),
           dma((FRONTS, CHUNKS)), dma((FRONTS, CHUNKS)), dma((FRONTS, CHUNKS)), dma((2,)), dma((2,))],
        compiler_params=pltpu.CompilerParams(
            collective_id=0, has_side_effects=True, vmem_limit_bytes=48 * 1024 * 1024),
    )(work, a, b, u, v, shift)


def solution(mesh):
    placed = (
        P("row", "col"),
        P("row", None, "col", None),
        P(None, "col", "row", None),
        P("row", None, "col", None),
        P("col", None, "row", None),
        P(),
    )
    return jax.shard_map(
        functools.partial(per_device, mesh.shape["row"], mesh.shape["col"]),
        mesh=mesh, in_specs=placed, out_specs=P("row", "col"), check_vma=False
    )
```

```python
import functools
import jax
import jax.numpy as jnp
from jax import lax
from jax.experimental import pallas as pl
from jax.experimental.pallas import tpu as pltpu
from jax.sharding import PartitionSpec as P

FRONTS = 3
CHUNKS = 8
LANES = 128
MESH = pl.DeviceIdType.MESH
BF = jnp.bfloat16
F32 = jnp.float32


def dot(left, right):
    return jnp.dot(left, right, preferred_element_type=F32)


def split(value):
    high = value.astype(BF)
    return high, (value - high.astype(F32)).astype(BF)


def lay_left(parts):
    high, low = parts
    return [high, high, low]


def lay_right(parts):
    high, low = parts
    return [high, low, high]


def product(lefts, rights):
    left = jnp.concatenate(sum(map(lay_left, lefts), []), axis=1)
    return dot(left, jnp.concatenate(sum(map(lay_right, rights), []), axis=0))


def kernel(rows, cols, first, work, a, b, u, v, shift, s,
           ubuf, vbuf, utop, ulow, vnear, vfar, y, xs, abuf, bbuf, xd, xa,
           loc, usend, urecv, vsend, vrecv, asend, arecv, aloc, bsend, brecv, bloc,
           dsend, xsend, fsend, ssend, xdrecv, xarecv, vpass, vgot):
    r = lax.axis_index("row")
    c = lax.axis_index("col")
    width = s.shape[0]
    half = width // 2
    hr = u.shape[2]
    hv = v.shape[2]
    ch = width // CHUNKS
    mine = r + c - first
    solver = (mine >= 0) & (mine < FRONTS)
    even = lax.rem(r, 2) == 0
    last = mine == FRONTS - 1
    blocks = width // LANES

    def remote(src, dst, ssem, rsem, to_row, to_col):
        return pltpu.make_async_remote_copy(
            src_ref=src, dst_ref=dst, send_sem=ssem, recv_sem=rsem,
            device_id=(to_row, to_col), device_id_type=MESH)

    def arrived(ref, sem):
        pltpu.make_async_copy(ref, ref, sem).wait()

    def span(count, body):
        def step(at, carry):
            body(at)
            return carry
        lax.fori_loop(0, count, step, 0)

    own_u = pl.ds(pl.multiple_of(c * hr, hr), hr)
    own_v = pl.ds(pl.multiple_of(r * hv, hv), hv)

    load_s = pltpu.make_async_copy(work, s, loc.at[0])
    load_u = pltpu.make_async_copy(u.at[0, 0], ubuf.at[own_u], loc.at[1])
    load_v = pltpu.make_async_copy(v.at[0, 0], vbuf.at[own_v], loc.at[2])
    load_s.start()

    @pl.when(solver)
    def _():
        for low in range(blocks):
            for high in range(low + 1, blocks):
                if low * LANES // half == high * LANES // half:
                    x, y = pl.ds(low * LANES, LANES), pl.ds(high * LANES, LANES)
                    ubuf[x, y] = jnp.zeros((LANES, LANES), F32)
                    vbuf[y, x] = jnp.zeros((LANES, LANES), F32)
        load_u.start()

    @pl.when(solver & (mine != 1))
    def _():
        load_v.start()

    barrier = pltpu.get_barrier_semaphore()

    def greet_row(at):
        @pl.when(at != r)
        def _():
            pl.semaphore_signal(barrier, inc=1, device_id=(at, c), device_id_type=MESH)

    def greet_col(at):
        @pl.when(at != c)
        def _():
            pl.semaphore_signal(barrier, inc=1, device_id=(r, at), device_id_type=MESH)

    span(rows, greet_row)
    span(cols, greet_col)
    pl.semaphore_wait(barrier, rows + cols - 2)

    def u_filled(at, body):
        reach = (at * hr + hr - 1) // LANES
        for block in range(blocks):
            @pl.when(reach == block)
            def _():
                body(pl.ds(0, (block + 1) * LANES))

    def v_filled(at, body):
        reach = at * hv // LANES
        for block in range(blocks):
            @pl.when(reach == block)
            def _():
                body(pl.ds(block * LANES, width - block * LANES))

    def factors(f, act):
        j = first + f - r

        @pl.when((j >= 0) & (j < cols) & (j != c))
        def _():
            u_filled(c, lambda part: act(remote(
                u.at[0, 0, :, part], ubuf.at[own_u, part], usend.at[f], urecv.at[c], r, j)))

        i = first + f - c

        @pl.when((f != 1) & (i >= 0) & (i < rows) & (i != r))
        def _():
            v_filled(r, lambda part: act(remote(
                v.at[0, 0, :, part], vbuf.at[own_v, part], vsend.at[f], vrecv.at[r], i, c)))

    def a_send(f, j, need, act, act_local):
        k = first + f - j

        @pl.when(need & (j != c))
        def _():
            act(remote(a.at[0, k], abuf.at[f, own_u], asend.at[f, j], arecv.at[f, c], r, j))

        @pl.when(need & (j == c))
        def _():
            act_local(pltpu.make_async_copy(a.at[0, k], abuf.at[f, own_u], aloc.at[f]))

    def b_send(f, l, need, act, act_local):
        i = first + f - l

        @pl.when(need & (i != r))
        def _():
            act(remote(b.at[l, 0], bbuf.at[f, own_v], bsend.at[f, l], brecv.at[f, r], i, c))

        @pl.when(need & (i == r))
        def _():
            act_local(pltpu.make_async_copy(b.at[l, 0], bbuf.at[f, own_v], bloc.at[f]))

    def near(f, act, act_local):
        j, i = first + f + 1 - r, first + f + 1 - c
        a_send(f, j, (j >= 0) & (j < cols) & (r >= 1), act, act_local)
        b_send(f, c - 1, (i >= 0) & (i < rows) & (c >= 1), act, act_local)

    def rest(f, act, act_local):
        def a_step(at):
            j = lax.rem(c + 1 + at, cols)
            a_send(f, j, (r + j > first + f + 1) & (first + f - j >= 0), act, act_local)

        def b_step(l):
            i = first + f - l
            b_send(f, l, (i >= 0) & (i < rows) & (c > l + 1), act, act_local)

        span(cols, a_step)
        span(cols, b_step)

    def start(copy):
        copy.start()

    def sent(copy):
        copy.wait_send()

    def nothing(copy):
        return None

    factors(0, start)
    load_s.wait()

    def send_ahead(paced):
        for f in range(1, FRONTS):
            if paced:
                factors(f - 1, sent)
                if f > 1:
                    near(f - 2, sent, nothing)
            factors(f, start)
            near(f - 1, start, start)
        if paced:
            factors(FRONTS - 1, sent)
            near(FRONTS - 2, sent, nothing)
        near(FRONTS - 1, start, start)

    @pl.when(mine != 0)
    def _():
        send_ahead(True)
        span(FRONTS, lambda f: rest(f, start, start))

    t, e = slice(0, half), slice(half, width)

    def prepare(buf, corner, scale, keep):
        x, z = corner
        parts = ((t, t), (e, e), corner)
        eye = (lax.broadcasted_iota(jnp.int32, (half, half), 0)
               == lax.broadcasted_iota(jnp.int32, (half, half), 1)).astype(F32)

        def squares(values):
            both = [split(value) for value in values]
            out = [product([both[at]], [both[at]]) for at in range(2)]
            first_at, second_at = (0, 1) if x == t else (1, 0)
            out.append(product([both[first_at], both[2]], [both[2], both[second_at]]))
            return out, both

        base = [buf[p, q] for p, q in parts]
        second, _ = squares(base)
        for at, part in enumerate(parts):
            keep(0, at, split(((eye - base[at]) if at < 2 else -base[at]) * scale))
            keep(1, at, split((base[at] - second[at]) * scale))
        fourth, both = squares(second)
        for at, part in enumerate(parts):
            keep(2, at, both[at])
            keep(3, at, split(fourth[at]))

    def keep_u(slot, at, parts):
        value = jnp.concatenate(lay_left(parts), axis=1)
        if at == 0:
            utop[slot] = value
        else:
            place = 3 * half * (2 - at)
            ulow[slot, :, place:place + 3 * half] = value

    def keep_v(slot, at, parts):
        value = jnp.concatenate(lay_right(parts), axis=0)
        if at == 0:
            vnear[slot * 3 * half:(slot + 1) * 3 * half, :] = value
        else:
            place = (2 * slot + 2 - at) * 3 * half
            vfar[place:place + 3 * half, :] = value

    @pl.when(solver)
    def _():
        load_u.wait()

        def u_wait(at):
            @pl.when(at != c)
            def _():
                place = pl.ds(pl.multiple_of(at * hr, hr), hr)
                u_filled(at, lambda part: arrived(ubuf.at[place, part], urecv.at[at]))

        span(cols, u_wait)
        prepare(ubuf, (e, t), 1.0, keep_u)

    @pl.when(mine == 0)
    def _():
        send_ahead(False)

    beside = jnp.where(even, r + 1, r - 1)
    passing = solver & (mine != 1) & ((mine == 0) == even)

    def pass_v(act):
        for at, (x, y) in enumerate(((t, t), (slice(0, width), e))):
            part = vbuf.at[pl.ds(x.start, x.stop - x.start), pl.ds(y.start, y.stop - y.start)]
            act(remote(part, part, vpass.at[at], vgot.at[at], beside, c))

    @pl.when(mine == 1)
    def _():
        pass_v(lambda copy: copy.wait_recv())

    @pl.when(solver & (mine != 1))
    def _():
        load_v.wait()

        def v_wait(at):
            @pl.when(at != r)
            def _():
                place = pl.ds(pl.multiple_of(at * hv, hv), hv)
                v_filled(at, lambda part: arrived(vbuf.at[place, part], vrecv.at[at]))

        span(rows, v_wait)

        @pl.when(passing)
        def _():
            pass_v(start)

    @pl.when(solver)
    def _():
        prepare(vbuf, (t, e), 0.5 / jnp.broadcast_to(shift[0], (1, half)).astype(F32), keep_v)

    def chunk(k):
        return pl.ds(pl.multiple_of(k * ch, ch), ch)

    def forwards(f, k, act):
        part = xd.at[f, chunk(k)]

        @pl.when(r + 1 < rows)
        def _():
            act(remote(part, part, fsend.at[f, k], xdrecv.at[f, k], r + 1, c))

    square = cols == 4

    def relays(f):
        source = first + f - r
        if not square:
            return source < 0
        return ((source == 0) & (c == 2)) | ((source == 1) & (c == 3) & (f == FRONTS - 1))

    def sideways(f, k, act):
        if square:
            part = xa.at[f, chunk(k)]

            @pl.when(relays(f))
            def _():
                act(remote(part, part, ssend.at[f, k], xarecv.at[f, k], r, 5 - c))

    def a_needed(f):
        return (mine > f) & (first + f - c >= 0)

    def b_needed(f):
        return (mine > f) & (first + f - r >= 0)

    def update(f):
        @pl.when(a_needed(f))
        def _():
            arrived(abuf.at[f, own_u], aloc.at[f])

            def a_wait(at):
                @pl.when(at != c)
                def _():
                    arrived(abuf.at[f, pl.ds(pl.multiple_of(at * hr, hr), hr)], arecv.at[f, at])

            span(cols, a_wait)

        @pl.when(b_needed(f))
        def _():
            arrived(bbuf.at[f, own_v], bloc.at[f])

            def b_wait(at):
                @pl.when(at != r)
                def _():
                    arrived(bbuf.at[f, pl.ds(pl.multiple_of(at * hv, hv), hv)], brecv.at[f, at])

            span(rows, b_wait)

        def d_wait(k):
            arrived(xd.at[f, chunk(k)], xdrecv.at[f, k])
            forwards(f, k, start)

        def x_wait(k):
            arrived(xa.at[f, chunk(k)], xarecv.at[f, k])
            sideways(f, k, start)

        relay = b_needed(f) & relays(f)

        @pl.when(relay)
        def _():
            span(CHUNKS, x_wait)

        @pl.when(a_needed(f))
        def _():
            span(CHUNKS, d_wait)
            s[...] -= dot(abuf[f], xd[f])

        @pl.when(b_needed(f) & jnp.logical_not(relay))
        def _():
            span(CHUNKS, x_wait)

        @pl.when(b_needed(f))
        def _():
            s[...] -= dot(xa[f], bbuf[f])

    span(FRONTS, update)

    def across(k, at, act):
        relayed = at < 0
        if square:
            relayed = ((c == 0) & (at == 3)) | ((c == 1) & (at == 1) & last)

        @pl.when((c + at < cols) & jnp.logical_not(relayed))
        def _():
            act(remote(xs.at[chunk(k)], xa.at[mine, chunk(k)], xsend.at[k, at - 1],
                       xarecv.at[mine, k], r, c + at))

    def spread(k, act):
        @pl.when(r + 1 < rows)
        def _():
            act(remote(xs.at[chunk(k)], xd.at[mine, chunk(k)], dsend.at[k],
                       xdrecv.at[mine, k], r + 1, c))

        across(k, 1, act)

        @pl.when(last)
        def _():
            span(cols - 2, lambda at: across(k, at + 2, act))

    def spread_late(act):
        @pl.when(solver & jnp.logical_not(last))
        def _():
            span(cols - 2, lambda at: span(CHUNKS, lambda k: across(k, at + 2, act)))

    @pl.when(solver)
    def _():
        def put(stage, at, value):
            y[stage, at * 3 * half:(at + 1) * 3 * half, :] = jnp.concatenate(
                lay_right(split(value)), axis=0)

        for at, part in enumerate((t, e)):
            put(0, at, s[part, :])

            def left(slot, stage):
                if at == 0:
                    moved = dot(utop[slot], y[stage, :3 * half, :])
                else:
                    moved = dot(ulow[slot], y[stage])
                high, low = split(moved)
                return lay_left((high[:, :half], low[:, :half])), lay_left((high[:, half:], low[:, half:]))

            def right(slot, moved):
                count = len(moved)
                near_part = jnp.concatenate(sum((m[0] for m in moved), []), axis=1)
                far_part = jnp.concatenate(sum((m[0] + m[1] for m in moved), []), axis=1)
                left_half = dot(near_part, vnear[slot * 3 * half:(slot + count) * 3 * half, :])
                right_half = dot(far_part, vfar[slot * 6 * half:(slot + count) * 6 * half, :])
                return jnp.concatenate([left_half, right_half], axis=1)

            now = right(0, [left(0, 0), left(1, 0)])
            for stage in (1, 2):
                put(stage, at, now)
                now = now + right(stage + 1, [left(stage + 1, stage)])
            s[part, :] = now
            xs[part, :] = now.astype(BF)
            lowest = part.start // ch

            span(CHUNKS // 2, lambda at: spread(lowest + at, start))

    spread_late(start)

    @pl.when(mine == 0)
    def _():
        span(FRONTS, lambda f: rest(f, start, start))

    @pl.when(mine == 0)
    def _():
        for f in range(FRONTS):
            factors(f, sent)
        for f in range(FRONTS - 1):
            near(f, sent, nothing)

    near(FRONTS - 1, sent, nothing)
    span(FRONTS, lambda f: rest(f, sent, nothing))

    def drain(f):
        @pl.when(a_needed(f))
        def _():
            span(CHUNKS, lambda k: forwards(f, k, sent))

        @pl.when(b_needed(f))
        def _():
            span(CHUNKS, lambda k: sideways(f, k, sent))

    span(FRONTS, drain)

    @pl.when(passing)
    def _():
        pass_v(sent)

    @pl.when(solver)
    def _():
        span(CHUNKS, lambda k: spread(k, sent))

    spread_late(sent)


def per_device(rows, cols, work, a, b, u, v, shift):
    first = max(0, (rows + cols) // 2 - FRONTS)
    width = work.shape[0]
    tile, half = (width, width), width // 2
    hbm_ref = pl.BlockSpec(memory_space=pltpu.HBM)
    work, a, b, u, v = (pltpu.with_memory_space_constraint(x, pltpu.HBM) for x in (work, a, b, u, v))
    dma = pltpu.SemaphoreType.DMA
    stack = [pltpu.VMEM((FRONTS,) + tile, BF)]
    return pl.pallas_call(
        functools.partial(kernel, rows, cols, first),
        out_shape=pltpu.VMEM(work.shape, work.dtype),
        in_specs=[hbm_ref] * 5 + [pl.BlockSpec(memory_space=pltpu.SMEM)],
        out_specs=pl.BlockSpec(memory_space=pltpu.VMEM),
        scratch_shapes=[pltpu.VMEM(tile, F32)] * 2 + [
            pltpu.VMEM((4, half, 3 * half), BF), pltpu.VMEM((4, half, 6 * half), BF),
            pltpu.VMEM((12 * half, half), BF), pltpu.VMEM((24 * half, half), BF),
            pltpu.VMEM((3, 6 * half, width), BF)]
        + [pltpu.VMEM(tile, BF)] + stack * 4
        + [dma((3,)), dma((FRONTS,)), dma((cols,)), dma((FRONTS,)), dma((rows,)),
           dma((FRONTS, cols)), dma((FRONTS, cols)), dma((FRONTS,)),
           dma((FRONTS, cols)), dma((FRONTS, rows)), dma((FRONTS,)),
           dma((CHUNKS,)), dma((CHUNKS, cols - 1)), dma((FRONTS, CHUNKS)),
           dma((FRONTS, CHUNKS)), dma((FRONTS, CHUNKS)), dma((FRONTS, CHUNKS)), dma((2,)), dma((2,))],
        compiler_params=pltpu.CompilerParams(
            collective_id=0, has_side_effects=True, vmem_limit_bytes=48 * 1024 * 1024),
    )(work, a, b, u, v, shift)


def solution(mesh):
    placed = (
        P("row", "col"),
        P("row", None, "col", None),
        P(None, "col", "row", None),
        P("row", None, "col", None),
        P("col", None, "row", None),
        P(),
    )
    return jax.shard_map(
        functools.partial(per_device, mesh.shape["row"], mesh.shape["col"]),
        mesh=mesh, in_specs=placed, out_specs=P("row", "col"), check_vma=False
    )
```

```python
import functools
import jax
import jax.numpy as jnp
from jax import lax
from jax.experimental import pallas as pl
from jax.experimental.pallas import tpu as pltpu
from jax.sharding import PartitionSpec as P

FRONTS = 3
CHUNKS = 8
LANES = 128
MESH = pl.DeviceIdType.MESH
BF = jnp.bfloat16
F32 = jnp.float32


def dot(left, right):
    return jnp.dot(left, right, preferred_element_type=F32)


def split(value):
    high = value.astype(BF)
    return high, (value - high.astype(F32)).astype(BF)


def lay_left(parts):
    high, low = parts
    return [high, high, low]


def lay_right(parts):
    high, low = parts
    return [high, low, high]


def product(lefts, rights):
    left = jnp.concatenate(sum(map(lay_left, lefts), []), axis=1)
    return dot(left, jnp.concatenate(sum(map(lay_right, rights), []), axis=0))


def kernel(rows, cols, first, work, a, b, u, v, shift, s,
           ubuf, vbuf, utop, ulow, vnear, vfar, y, xs, abuf, bbuf, xd, xa,
           loc, usend, urecv, vsend, vrecv, asend, arecv, aloc, bsend, brecv, bloc,
           dsend, xsend, fsend, ssend, xdrecv, xarecv, vpass, vgot):
    r = lax.axis_index("row")
    c = lax.axis_index("col")
    width = s.shape[0]
    half = width // 2
    hr = u.shape[2]
    hv = v.shape[2]
    ch = width // CHUNKS
    mine = r + c - first
    solver = (mine >= 0) & (mine < FRONTS)
    even = lax.rem(r, 2) == 0
    last = mine == FRONTS - 1
    blocks = width // LANES

    def remote(src, dst, ssem, rsem, to_row, to_col):
        return pltpu.make_async_remote_copy(
            src_ref=src, dst_ref=dst, send_sem=ssem, recv_sem=rsem,
            device_id=(to_row, to_col), device_id_type=MESH)

    def arrived(ref, sem):
        pltpu.make_async_copy(ref, ref, sem).wait()

    def span(count, body):
        def step(at, carry):
            body(at)
            return carry
        lax.fori_loop(0, count, step, 0)

    own_u = pl.ds(pl.multiple_of(c * hr, hr), hr)
    own_v = pl.ds(pl.multiple_of(r * hv, hv), hv)

    load_s = pltpu.make_async_copy(work, s, loc.at[0])
    load_u = pltpu.make_async_copy(u.at[0, 0], ubuf.at[own_u], loc.at[1])
    load_v = pltpu.make_async_copy(v.at[0, 0], vbuf.at[own_v], loc.at[2])
    load_s.start()

    @pl.when(solver)
    def _():
        for low in range(blocks):
            for high in range(low + 1, blocks):
                if low * LANES // half == high * LANES // half:
                    x, y = pl.ds(low * LANES, LANES), pl.ds(high * LANES, LANES)
                    ubuf[x, y] = jnp.zeros((LANES, LANES), F32)
                    vbuf[y, x] = jnp.zeros((LANES, LANES), F32)
        load_u.start()

    @pl.when(solver & (mine != 1))
    def _():
        load_v.start()

    barrier = pltpu.get_barrier_semaphore()

    def greet_row(at):
        @pl.when(at != r)
        def _():
            pl.semaphore_signal(barrier, inc=1, device_id=(at, c), device_id_type=MESH)

    def greet_col(at):
        @pl.when(at != c)
        def _():
            pl.semaphore_signal(barrier, inc=1, device_id=(r, at), device_id_type=MESH)

    span(rows, greet_row)
    span(cols, greet_col)
    pl.semaphore_wait(barrier, rows + cols - 2)

    def u_filled(at, body):
        reach = (at * hr + hr - 1) // LANES
        for block in range(blocks):
            @pl.when(reach == block)
            def _():
                body(pl.ds(0, (block + 1) * LANES))

    def v_filled(at, body):
        reach = at * hv // LANES
        for block in range(blocks):
            @pl.when(reach == block)
            def _():
                body(pl.ds(block * LANES, width - block * LANES))

    def factors(f, act):
        j = first + f - r

        @pl.when((j >= 0) & (j < cols) & (j != c))
        def _():
            u_filled(c, lambda part: act(remote(
                u.at[0, 0, :, part], ubuf.at[own_u, part], usend.at[f], urecv.at[c], r, j)))

        i = first + f - c

        @pl.when((f != 1) & (i >= 0) & (i < rows) & (i != r))
        def _():
            v_filled(r, lambda part: act(remote(
                v.at[0, 0, :, part], vbuf.at[own_v, part], vsend.at[f], vrecv.at[r], i, c)))

    def a_send(f, j, need, act, act_local):
        k = first + f - j

        @pl.when(need & (j != c))
        def _():
            act(remote(a.at[0, k], abuf.at[f, own_u], asend.at[f, j], arecv.at[f, c], r, j))

        @pl.when(need & (j == c))
        def _():
            act_local(pltpu.make_async_copy(a.at[0, k], abuf.at[f, own_u], aloc.at[f]))

    def b_send(f, l, need, act, act_local):
        i = first + f - l

        @pl.when(need & (i != r))
        def _():
            act(remote(b.at[l, 0], bbuf.at[f, own_v], bsend.at[f, l], brecv.at[f, r], i, c))

        @pl.when(need & (i == r))
        def _():
            act_local(pltpu.make_async_copy(b.at[l, 0], bbuf.at[f, own_v], bloc.at[f]))

    def near(f, act, act_local):
        j, i = first + f + 1 - r, first + f + 1 - c
        a_send(f, j, (j >= 0) & (j < cols) & (r >= 1), act, act_local)
        b_send(f, c - 1, (i >= 0) & (i < rows) & (c >= 1), act, act_local)

    def rest(f, act, act_local):
        def a_step(at):
            j = lax.rem(c + 1 + at, cols)
            a_send(f, j, (r + j > first + f + 1) & (first + f - j >= 0), act, act_local)

        def b_step(l):
            i = first + f - l
            b_send(f, l, (i >= 0) & (i < rows) & (c > l + 1), act, act_local)

        span(cols, a_step)
        span(cols, b_step)

    def start(copy):
        copy.start()

    def sent(copy):
        copy.wait_send()

    def nothing(copy):
        return None

    factors(0, start)
    load_s.wait()

    def send_ahead(paced):
        for f in range(1, FRONTS):
            if paced:
                factors(f - 1, sent)
                if f > 1:
                    near(f - 2, sent, nothing)
            factors(f, start)
            near(f - 1, start, start)
        if paced:
            factors(FRONTS - 1, sent)
            near(FRONTS - 2, sent, nothing)
        near(FRONTS - 1, start, start)

    @pl.when(mine != 0)
    def _():
        send_ahead(True)
        span(FRONTS, lambda f: rest(f, start, start))

    t, e = slice(0, half), slice(half, width)

    def prepare(buf, corner, scale, keep):
        x, z = corner
        parts = ((t, t), (e, e), corner)
        eye = (lax.broadcasted_iota(jnp.int32, (half, half), 0)
               == lax.broadcasted_iota(jnp.int32, (half, half), 1)).astype(F32)

        def squares(values):
            both = [split(value) for value in values]
            out = [product([both[at]], [both[at]]) for at in range(2)]
            first_at, second_at = (0, 1) if x == t else (1, 0)
            out.append(product([both[first_at], both[2]], [both[2], both[second_at]]))
            return out, both

        base = [buf[p, q] for p, q in parts]
        second, _ = squares(base)
        for at, part in enumerate(parts):
            keep(0, at, split(((eye - base[at]) if at < 2 else -base[at]) * scale))
            keep(1, at, split((base[at] - second[at]) * scale))
        fourth, both = squares(second)
        for at, part in enumerate(parts):
            keep(2, at, both[at])
            keep(3, at, split(fourth[at]))

    def keep_u(slot, at, parts):
        value = jnp.concatenate(lay_left(parts), axis=1)
        if at == 0:
            utop[slot] = value
        else:
            place = 3 * half * (2 - at)
            ulow[slot, :, place:place + 3 * half] = value

    def keep_v(slot, at, parts):
        value = jnp.concatenate(lay_right(parts), axis=0)
        if at == 0:
            vnear[slot * 3 * half:(slot + 1) * 3 * half, :] = value
        else:
            place = (2 * slot + 2 - at) * 3 * half
            vfar[place:place + 3 * half, :] = value

    @pl.when(solver)
    def _():
        load_u.wait()

        def u_wait(at):
            @pl.when(at != c)
            def _():
                place = pl.ds(pl.multiple_of(at * hr, hr), hr)
                u_filled(at, lambda part: arrived(ubuf.at[place, part], urecv.at[at]))

        span(cols, u_wait)
        prepare(ubuf, (e, t), 1.0, keep_u)

    @pl.when(mine == 0)
    def _():
        send_ahead(False)

    beside = jnp.where(even, r + 1, r - 1)
    passing = solver & (mine != 1) & ((mine == 0) == even)

    def pass_v(act):
        for at, (x, y) in enumerate(((t, t), (slice(0, width), e))):
            part = vbuf.at[pl.ds(x.start, x.stop - x.start), pl.ds(y.start, y.stop - y.start)]
            act(remote(part, part, vpass.at[at], vgot.at[at], beside, c))

    @pl.when(mine == 1)
    def _():
        pass_v(lambda copy: copy.wait_recv())

    @pl.when(solver & (mine != 1))
    def _():
        load_v.wait()

        def v_wait(at):
            @pl.when(at != r)
            def _():
                place = pl.ds(pl.multiple_of(at * hv, hv), hv)
                v_filled(at, lambda part: arrived(vbuf.at[place, part], vrecv.at[at]))

        span(rows, v_wait)

        @pl.when(passing)
        def _():
            pass_v(start)

    @pl.when(solver)
    def _():
        prepare(vbuf, (t, e), 0.5 / jnp.broadcast_to(shift[0], (1, half)).astype(F32), keep_v)

    def chunk(k):
        return pl.ds(pl.multiple_of(k * ch, ch), ch)

    def forwards(f, k, act):
        part = xd.at[f, chunk(k)]

        @pl.when(r + 1 < rows)
        def _():
            act(remote(part, part, fsend.at[f, k], xdrecv.at[f, k], r + 1, c))

    square = cols == 4

    def relays(f):
        source = first + f - r
        if not square:
            return source < 0
        return (((source == 0) & (c == 2)) | ((source == 1) & (c == 3))) & (f == FRONTS - 1)

    def sideways(f, k, act):
        if square:
            part = xa.at[f, chunk(k)]

            @pl.when(relays(f))
            def _():
                act(remote(part, part, ssend.at[f, k], xarecv.at[f, k], r, 5 - c))

    def a_needed(f):
        return (mine > f) & (first + f - c >= 0)

    def b_needed(f):
        return (mine > f) & (first + f - r >= 0)

    def update(f):
        @pl.when(a_needed(f))
        def _():
            arrived(abuf.at[f, own_u], aloc.at[f])

            def a_wait(at):
                @pl.when(at != c)
                def _():
                    arrived(abuf.at[f, pl.ds(pl.multiple_of(at * hr, hr), hr)], arecv.at[f, at])

            span(cols, a_wait)

        @pl.when(b_needed(f))
        def _():
            arrived(bbuf.at[f, own_v], bloc.at[f])

            def b_wait(at):
                @pl.when(at != r)
                def _():
                    arrived(bbuf.at[f, pl.ds(pl.multiple_of(at * hv, hv), hv)], brecv.at[f, at])

            span(rows, b_wait)

        def d_wait(k):
            arrived(xd.at[f, chunk(k)], xdrecv.at[f, k])
            forwards(f, k, start)

        def x_wait(k):
            arrived(xa.at[f, chunk(k)], xarecv.at[f, k])
            sideways(f, k, start)

        relay = b_needed(f) & relays(f)

        @pl.when(relay)
        def _():
            span(CHUNKS, x_wait)

        @pl.when(a_needed(f))
        def _():
            span(CHUNKS, d_wait)
            s[...] -= dot(abuf[f], xd[f])

        @pl.when(b_needed(f) & jnp.logical_not(relay))
        def _():
            span(CHUNKS, x_wait)

        @pl.when(b_needed(f))
        def _():
            s[...] -= dot(xa[f], bbuf[f])

    span(FRONTS, update)

    def across(k, at, act):
        relayed = at < 0
        if square:
            relayed = (((c == 0) & (at == 3)) | ((c == 1) & (at == 1))) & last

        @pl.when((c + at < cols) & jnp.logical_not(relayed))
        def _():
            act(remote(xs.at[chunk(k)], xa.at[mine, chunk(k)], xsend.at[k, at - 1],
                       xarecv.at[mine, k], r, c + at))

    def spread(k, act):
        @pl.when(r + 1 < rows)
        def _():
            act(remote(xs.at[chunk(k)], xd.at[mine, chunk(k)], dsend.at[k],
                       xdrecv.at[mine, k], r + 1, c))

        across(k, 1, act)

        @pl.when(last)
        def _():
            span(cols - 2, lambda at: across(k, at + 2, act))

    def spread_late(act):
        @pl.when(solver & jnp.logical_not(last))
        def _():
            span(cols - 2, lambda at: span(CHUNKS, lambda k: across(k, at + 2, act)))

    @pl.when(solver)
    def _():
        def put(stage, at, value):
            y[stage, at * 3 * half:(at + 1) * 3 * half, :] = jnp.concatenate(
                lay_right(split(value)), axis=0)

        for at, part in enumerate((t, e)):
            put(0, at, s[part, :])

            def left(slot, stage):
                if at == 0:
                    moved = dot(utop[slot], y[stage, :3 * half, :])
                else:
                    moved = dot(ulow[slot], y[stage])
                high, low = split(moved)
                return lay_left((high[:, :half], low[:, :half])), lay_left((high[:, half:], low[:, half:]))

            def right(slot, moved):
                count = len(moved)
                near_part = jnp.concatenate(sum((m[0] for m in moved), []), axis=1)
                far_part = jnp.concatenate(sum((m[0] + m[1] for m in moved), []), axis=1)
                left_half = dot(near_part, vnear[slot * 3 * half:(slot + count) * 3 * half, :])
                right_half = dot(far_part, vfar[slot * 6 * half:(slot + count) * 6 * half, :])
                return jnp.concatenate([left_half, right_half], axis=1)

            now = right(0, [left(0, 0), left(1, 0)])
            for stage in (1, 2):
                put(stage, at, now)
                now = now + right(stage + 1, [left(stage + 1, stage)])
            s[part, :] = now
            xs[part, :] = now.astype(BF)
            lowest = part.start // ch

            span(CHUNKS // 2, lambda at: spread(lowest + at, start))

    spread_late(start)

    @pl.when(mine == 0)
    def _():
        span(FRONTS, lambda f: rest(f, start, start))

    @pl.when(mine == 0)
    def _():
        for f in range(FRONTS):
            factors(f, sent)
        for f in range(FRONTS - 1):
            near(f, sent, nothing)

    near(FRONTS - 1, sent, nothing)
    span(FRONTS, lambda f: rest(f, sent, nothing))

    def drain(f):
        @pl.when(a_needed(f))
        def _():
            span(CHUNKS, lambda k: forwards(f, k, sent))

        @pl.when(b_needed(f))
        def _():
            span(CHUNKS, lambda k: sideways(f, k, sent))

    span(FRONTS, drain)

    @pl.when(passing)
    def _():
        pass_v(sent)

    @pl.when(solver)
    def _():
        span(CHUNKS, lambda k: spread(k, sent))

    spread_late(sent)


def per_device(rows, cols, work, a, b, u, v, shift):
    first = max(0, (rows + cols) // 2 - FRONTS)
    width = work.shape[0]
    tile, half = (width, width), width // 2
    hbm_ref = pl.BlockSpec(memory_space=pltpu.HBM)
    work, a, b, u, v = (pltpu.with_memory_space_constraint(x, pltpu.HBM) for x in (work, a, b, u, v))
    dma = pltpu.SemaphoreType.DMA
    stack = [pltpu.VMEM((FRONTS,) + tile, BF)]
    return pl.pallas_call(
        functools.partial(kernel, rows, cols, first),
        out_shape=pltpu.VMEM(work.shape, work.dtype),
        in_specs=[hbm_ref] * 5 + [pl.BlockSpec(memory_space=pltpu.SMEM)],
        out_specs=pl.BlockSpec(memory_space=pltpu.VMEM),
        scratch_shapes=[pltpu.VMEM(tile, F32)] * 2 + [
            pltpu.VMEM((4, half, 3 * half), BF), pltpu.VMEM((4, half, 6 * half), BF),
            pltpu.VMEM((12 * half, half), BF), pltpu.VMEM((24 * half, half), BF),
            pltpu.VMEM((3, 6 * half, width), BF)]
        + [pltpu.VMEM(tile, BF)] + stack * 4
        + [dma((3,)), dma((FRONTS,)), dma((cols,)), dma((FRONTS,)), dma((rows,)),
           dma((FRONTS, cols)), dma((FRONTS, cols)), dma((FRONTS,)),
           dma((FRONTS, cols)), dma((FRONTS, rows)), dma((FRONTS,)),
           dma((CHUNKS,)), dma((CHUNKS, cols - 1)), dma((FRONTS, CHUNKS)),
           dma((FRONTS, CHUNKS)), dma((FRONTS, CHUNKS)), dma((FRONTS, CHUNKS)), dma((2,)), dma((2,))],
        compiler_params=pltpu.CompilerParams(
            collective_id=0, has_side_effects=True, vmem_limit_bytes=48 * 1024 * 1024),
    )(work, a, b, u, v, shift)


def solution(mesh):
    placed = (
        P("row", "col"),
        P("row", None, "col", None),
        P(None, "col", "row", None),
        P("row", None, "col", None),
        P("col", None, "row", None),
        P(),
    )
    return jax.shard_map(
        functools.partial(per_device, mesh.shape["row"], mesh.shape["col"]),
        mesh=mesh, in_specs=placed, out_specs=P("row", "col"), check_vma=False
    )
```
